32 devices in a mesh: tr: 4 (over x, core), gz: 8 (over z, y).
Axes of the slice: x: 2, y: 2, z: 4, core: 2. Of those that a mesh axis runs over, the one named last changes fastest.
Arguments:
- tokens: bfloat16 [40, 32, 8, 768], P('gz', None, 'tr'), may hold values from -6 to 6
- cotangent: bfloat16 [40, 32, 8, 768], P('gz', None, 'tr'), may hold values from -6 to 6
- gain_x: float32 [768], replicated, may hold values from 0.1 to 1.9
- wqkv_x: bfloat16 [768, 2304], P('tr'), as said below
- wo_x: bfloat16 [768, 768], P('tr'), may hold values from -0.21875 to 0.21875
- gain_z: float32 [768], replicated, may hold values from 0.1 to 1.9
- wqkv_z: bfloat16 [768, 2304], P('tr'), as said below
- wo_z: bfloat16 [768, 768], P('tr'), may hold values from -0.21875 to 0.21875
Outputs:
- grad_tokens: bfloat16 [40, 32, 8, 768], P('gz', None, 'tr')
The draws below stay inside these ranges and needn't reach their ends.
Inputs may be any that keep to these rules, and one draw needn't show every extreme that they name: `wqkv_x`: query, key and value columns side by side, each block split into 6 heads of 128. `wqkv_z`: query, key and value columns side by side, each block split into 6 heads of 128.
All inputs are finite; a program needn't handle non-finite values.
Results may differ from the reference program's by a relative error of at most 0.038.
The reference program's roundings to bfloat16 on the way count: a program that leaves them out, or rounds other values in their place, can miss the bound.
Values may be sent and summed in bfloat16 or wider, within the bound.
A program may use at most 64 MiB of HBM per device.

```python
import jax
import jax.numpy as jnp
from jax import lax

H = 6
HD = 128
D = 768
Y = 32
X = 8
Z = 40


def projection_draw(key):
    base = jnp.clip(jax.random.normal(key, (D, 3 * D), jnp.float32), -6.0, 6.0) * D ** (-0.5)
    return base


def draw_wqkv_x(key, part):
    return projection_draw(jax.random.fold_in(key, 3)).astype(jnp.bfloat16)


def draw_wqkv_z(key, part):
    return projection_draw(jax.random.fold_in(key, 5)).astype(jnp.bfloat16)


def level_of(rng, extent, split, least, top_value):
    factor_of, own = 1.0, jax.random.fold_in(rng, 6)
    for dim, shards_of in split:
        heights = jnp.exp(jax.random.uniform(jax.random.fold_in(own, dim), (shards_of,), jnp.float32, least / len(split), top_value / len(split)))
        factor_of = factor_of * jnp.repeat(heights, extent[dim] // shards_of).reshape([-1 if axis == dim else 1 for axis in range(len(extent))])
    return factor_of


def gaussian(stream_key, dims, width, bound, shards=(), kind=jnp.bfloat16):
    result = jax.random.normal(stream_key, dims, jnp.float32) * width
    if len(shards) > 0:
        result = level_of(stream_key, dims, shards, -0.22, 0.18) * result
    return jnp.clip(result, min=-bound, max=bound).astype(kind)


def setup_inputs(seed: int = 0) -> dict:
    keys = jax.random.split(jax.random.key(seed), 9)
    return {
        "tokens": gaussian(keys[0], (Z, Y, X, D), 1.0, 6.0, ((0, 8), (2, 4))),
        "cotangent": gaussian(keys[1], (Z, Y, X, D), 1.0, 6.0, ((0, 8), (2, 4))),
        "gain_x": jnp.clip(1.0 + 0.18 * jax.random.normal(keys[2], (D,), jnp.float32), 0.1, 1.9),
        "wqkv_x": draw_wqkv_x(jax.random.fold_in(keys[8], 71), 0),
        "wo_x": gaussian(keys[4], (D, D), D ** -0.5, 0.21875, ((0, 4),)),
        "gain_z": jnp.clip(1.0 + 0.18 * jax.random.normal(keys[5], (D,), jnp.float32), 0.1, 1.9),
        "wqkv_z": draw_wqkv_z(jax.random.fold_in(keys[8], 71), 0),
        "wo_z": gaussian(keys[7], (D, D), D ** -0.5, 0.21875, ((0, 4),)),
    }


def rounded(value):
    return lax.optimization_barrier(value.astype(jnp.bfloat16))

def head_split(packed, index):
    width_all = packed.shape[-1] // 3
    piece = packed[..., index * width_all:(index + 1) * width_all]
    return piece.reshape(piece.shape[:-1] + (H, HD))

def merge_heads(value):
    return value.reshape(value.shape[:-2] + (H * HD,))

def recompute(tokens_in, gain_vec, w_in, layout):
    widened = tokens_in.astype(jnp.float32)
    inv_rms = lax.rsqrt(lax.optimization_barrier(jnp.mean(widened * widened, axis=-1, keepdims=True)) + 1e-06)
    normed = rounded(widened * inv_rms * gain_vec)
    packed = rounded(jnp.dot(normed, w_in, preferred_element_type=jnp.float32))
    queries = head_split(packed, 0).astype(jnp.float32)
    key_part = head_split(packed, 1).astype(jnp.float32)
    values = head_split(packed, 2).astype(jnp.float32)
    key_form = layout.replace('l', 'm')
    scores = jnp.einsum(layout + ',' + key_form + '->bhlm', queries, key_part) * HD ** (-0.5)
    probs = jax.nn.softmax(scores, axis=-1)
    probs_b = rounded(probs).astype(jnp.float32)
    return (widened, inv_rms, queries, key_part, values, probs, probs_b)

def forward_out(tokens_in, gain_vec, w_in, w_out, layout):
    widened, inv_rms, queries, key_part, values, probs, probs_b = recompute(tokens_in, gain_vec, w_in, layout)
    key_form = layout.replace('l', 'm')
    mixed = rounded(merge_heads(jnp.einsum('bhlm,' + key_form + '->' + layout, probs_b, values)))
    return (widened + jnp.dot(mixed, w_out, preferred_element_type=jnp.float32)).astype(jnp.bfloat16)

def backward(tokens_in, upstream, gain_vec, w_in, w_out, layout):
    widened, inv_rms, queries, key_part, values, probs, probs_b = recompute(tokens_in, gain_vec, w_in, layout)
    key_form = layout.replace('l', 'm')
    d_mixed = rounded(jnp.dot(upstream, w_out.T, preferred_element_type=jnp.float32))
    d_mixed = d_mixed.reshape(d_mixed.shape[:-1] + (H, HD)).astype(jnp.float32)
    d_probs = jnp.einsum(layout + ',' + key_form + '->bhlm', d_mixed, values)
    d_values = rounded(jnp.einsum('bhlm,' + layout + '->' + key_form, probs_b, d_mixed))
    centre = lax.optimization_barrier(jnp.sum(probs * d_probs, axis=-1, keepdims=True))
    d_scores = rounded(probs * (d_probs - centre) * HD ** (-0.5)).astype(jnp.float32)
    d_queries = rounded(jnp.einsum('bhlm,' + key_form + '->' + layout, d_scores, key_part))
    d_keys = rounded(jnp.einsum('bhlm,' + layout + '->' + key_form, d_scores, queries))
    joined = jnp.concatenate([merge_heads(d_queries), merge_heads(d_keys), merge_heads(d_values)], axis=-1)
    d_normed = jnp.dot(joined, w_in.T, preferred_element_type=jnp.float32)
    scaled = d_normed * gain_vec
    d_tokens = inv_rms * (scaled - widened * inv_rms * inv_rms * lax.optimization_barrier(jnp.mean(scaled * widened, axis=-1, keepdims=True)))
    return (upstream.astype(jnp.float32) + d_tokens).astype(jnp.bfloat16)

def reference(tokens, cotangent, gain_x, wqkv_x, wo_x, gain_z, wqkv_z, wo_z):
    mid = lax.map(lambda plane: forward_out(plane, gain_x, wqkv_x, wo_x, 'blhe'), tokens)
    columns = jnp.transpose(mid, (1, 0, 2, 3))
    cot_columns = jnp.transpose(cotangent, (1, 0, 2, 3))
    grad_columns = lax.map(lambda pair: backward(pair[0], pair[1], gain_z, wqkv_z, wo_z, 'lbhe'), (columns, cot_columns))
    grad_mid = jnp.transpose(grad_columns, (1, 0, 2, 3))
    return lax.map(lambda pair: backward(pair[0], pair[1], gain_x, wqkv_x, wo_x, 'blhe'), (tokens, grad_mid))
```

```python
import math

import jax
import jax.numpy as jnp
from jax import lax
from jax.sharding import PartitionSpec as P

H = 6


def head_split(packed, index, model_width):
    piece = packed[..., index * model_width : (index + 1) * model_width]
    return piece.reshape(piece.shape[:-1] + (H, model_width // H))


def merge_heads(value):
    return value.reshape(value.shape[:-2] + (value.shape[-2] * value.shape[-1],))


def recompute(tokens_in, gain_vec, w_in, layout):
    model_width = w_in.shape[0]
    factor = 1.0 / math.sqrt(model_width // H)
    widened = tokens_in.astype(jnp.float32)
    inv_rms = lax.rsqrt(jnp.mean(widened * widened, axis=-1, keepdims=True) + 1e-06)
    normed = (widened * inv_rms * gain_vec).astype(jnp.bfloat16)
    packed = jnp.dot(normed, w_in, preferred_element_type=jnp.float32).astype(jnp.bfloat16)
    queries = head_split(packed, 0, model_width)
    key_part = head_split(packed, 1, model_width)
    values = head_split(packed, 2, model_width)
    key_form = layout.replace("l", "m")
    scores = (
        jnp.einsum(
            layout + "," + key_form + "->bhlm",
            queries,
            key_part,
            preferred_element_type=jnp.float32,
        )
        * factor
    )
    highest = jnp.max(scores, axis=-1, keepdims=True)
    expanded = jnp.exp(scores - highest)
    probs = expanded / jnp.sum(expanded, axis=-1, keepdims=True)
    return (widened, inv_rms, queries, key_part, values, probs, probs.astype(jnp.bfloat16), factor)


def forward_out(tokens_in, gain_vec, w_in, w_out, layout):
    widened, inv_rms, queries, key_part, values, probs, probs_b, factor = recompute(
        tokens_in, gain_vec, w_in, layout
    )
    key_form = layout.replace("l", "m")
    mixed = jnp.einsum(
        "bhlm," + key_form + "->" + layout, probs_b, values, preferred_element_type=jnp.float32
    )
    mixed = merge_heads(mixed.astype(jnp.bfloat16))
    return (widened + jnp.dot(mixed, w_out, preferred_element_type=jnp.float32)).astype(
        jnp.bfloat16
    )


def backward(tokens_in, upstream, gain_vec, w_in, w_out, layout):
    widened, inv_rms, queries, key_part, values, probs, probs_b, factor = recompute(
        tokens_in, gain_vec, w_in, layout
    )
    key_form = layout.replace("l", "m")
    d_mixed = jnp.dot(upstream, w_out.T, preferred_element_type=jnp.float32).astype(jnp.bfloat16)
    d_mixed = d_mixed.reshape(d_mixed.shape[:-1] + (H, d_mixed.shape[-1] // H))
    d_probs = jnp.einsum(
        layout + "," + key_form + "->bhlm", d_mixed, values, preferred_element_type=jnp.float32
    )
    d_values = jnp.einsum(
        "bhlm," + layout + "->" + key_form, probs_b, d_mixed, preferred_element_type=jnp.float32
    ).astype(jnp.bfloat16)
    centre = jnp.sum(probs * d_probs, axis=-1, keepdims=True)
    d_scores = (probs * (d_probs - centre) * factor).astype(jnp.bfloat16)
    d_queries = jnp.einsum(
        "bhlm," + key_form + "->" + layout, d_scores, key_part, preferred_element_type=jnp.float32
    ).astype(jnp.bfloat16)
    d_keys = jnp.einsum(
        "bhlm," + layout + "->" + key_form, d_scores, queries, preferred_element_type=jnp.float32
    ).astype(jnp.bfloat16)
    joined = jnp.concatenate(
        [merge_heads(d_queries), merge_heads(d_keys), merge_heads(d_values)], axis=-1
    )
    d_normed = jnp.dot(joined, w_in.T, preferred_element_type=jnp.float32)
    scaled = d_normed * gain_vec
    d_tokens = inv_rms * (
        scaled - widened * inv_rms * inv_rms * jnp.mean(scaled * widened, axis=-1, keepdims=True)
    )
    return (upstream.astype(jnp.float32) + d_tokens).astype(jnp.bfloat16)


def line_forward(lines, gain_vec, w_in, w_out):
    feature_count = lines.shape[3]
    flat = lines.reshape(-1, lines.shape[2], feature_count)
    return forward_out(flat, gain_vec, w_in, w_out, "blhe").reshape(lines.shape)


def line_backward(lines, upstream, gain_vec, w_in, w_out):
    feature_count = lines.shape[3]
    flat = lines.reshape(-1, lines.shape[2], feature_count)
    flat_up = upstream.reshape(flat.shape)
    return backward(flat, flat_up, gain_vec, w_in, w_out, "blhe").reshape(lines.shape)


def per_device(tokens, cotangent, gain_x, wqkv_x, wo_x, gain_z, wqkv_z, wo_z):
    full_in_x, full_out_x = (
        lax.all_gather(wqkv_x, "tr", axis=0, tiled=True),
        lax.all_gather(wo_x, "tr", axis=0, tiled=True),
    )
    full_in_z, full_out_z = (
        lax.all_gather(wqkv_z, "tr", axis=0, tiled=True),
        lax.all_gather(wo_z, "tr", axis=0, tiled=True),
    )
    width = tokens.shape[-1]
    lines = lax.all_to_all(tokens, "tr", split_axis=1, concat_axis=2, tiled=True)
    cot_lines = lax.all_to_all(cotangent, "tr", split_axis=1, concat_axis=2, tiled=True)
    cells = lines.shape[1] * lines.shape[2]
    flat = (lines.shape[0], cells, width)
    cot_columns = lax.all_to_all(
        cot_lines.reshape(flat), "gz", split_axis=1, concat_axis=0, tiled=True
    )
    mid_lines = line_forward(lines, gain_x, full_in_x, full_out_x)
    mid_columns = lax.all_to_all(
        mid_lines.reshape(flat), "gz", split_axis=1, concat_axis=0, tiled=True
    )
    grad_columns = backward(
        mid_columns, cot_columns, gain_z, full_in_z, full_out_z, "lbhe"
    )
    grad_lines = lax.all_to_all(grad_columns, "gz", split_axis=0, concat_axis=1, tiled=True)
    result_lines = line_backward(lines, grad_lines.reshape(lines.shape), gain_x, full_in_x, full_out_x)
    return lax.all_to_all(result_lines, "tr", split_axis=2, concat_axis=1, tiled=True)


def solution(mesh):
    return jax.shard_map(
        per_device,
        mesh=mesh,
        in_specs=(
            P("gz", None, "tr", None),
            P("gz", None, "tr", None),
            P(),
            P("tr", None),
            P("tr", None),
            P(),
            P("tr", None),
            P("tr", None),
        ),
        out_specs=P("gz", None, "tr", None),
        check_vma=False,
    )
```

```python
import functools
import math

import jax
import jax.numpy as jnp
import numpy as np
from jax import lax
from jax.experimental import pallas as pl
from jax.experimental.pallas import tpu as pltpu
from jax.sharding import PartitionSpec as P

H = 6


def head_split(packed, index, model_width):
    piece = packed[..., index * model_width : (index + 1) * model_width]
    return piece.reshape(piece.shape[:-1] + (H, model_width // H))


def merge_heads(value):
    return value.reshape(value.shape[:-2] + (value.shape[-2] * value.shape[-1],))


def recompute(tokens_in, gain_vec, w_in, layout):
    model_width = w_in.shape[0]
    factor = 1.0 / math.sqrt(model_width // H)
    widened = tokens_in.astype(jnp.float32)
    inv_rms = lax.rsqrt(jnp.mean(widened * widened, axis=-1, keepdims=True) + 1e-06)
    normed = (widened * inv_rms * gain_vec).astype(jnp.bfloat16)
    packed = jnp.dot(normed, w_in, preferred_element_type=jnp.float32).astype(jnp.bfloat16)
    queries = head_split(packed, 0, model_width)
    key_part = head_split(packed, 1, model_width)
    values = head_split(packed, 2, model_width)
    key_form = layout.replace("l", "m")
    scores = (
        jnp.einsum(
            layout + "," + key_form + "->bhlm",
            queries,
            key_part,
            preferred_element_type=jnp.float32,
        )
        * factor
    )
    highest = jnp.max(scores, axis=-1, keepdims=True)
    expanded = jnp.exp(scores - highest)
    probs = expanded / jnp.sum(expanded, axis=-1, keepdims=True)
    return (widened, inv_rms, queries, key_part, values, probs, probs.astype(jnp.bfloat16), factor)


def forward_out(tokens_in, gain_vec, w_in, w_out, layout):
    widened, inv_rms, queries, key_part, values, probs, probs_b, factor = recompute(
        tokens_in, gain_vec, w_in, layout
    )
    key_form = layout.replace("l", "m")
    mixed = jnp.einsum(
        "bhlm," + key_form + "->" + layout, probs_b, values, preferred_element_type=jnp.float32
    )
    mixed = merge_heads(mixed.astype(jnp.bfloat16))
    return (widened + jnp.dot(mixed, w_out, preferred_element_type=jnp.float32)).astype(
        jnp.bfloat16
    )


def backward(tokens_in, upstream, gain_vec, w_in, w_out, layout):
    widened, inv_rms, queries, key_part, values, probs, probs_b, factor = recompute(
        tokens_in, gain_vec, w_in, layout
    )
    key_form = layout.replace("l", "m")
    d_mixed = jnp.dot(upstream, w_out.T, preferred_element_type=jnp.float32).astype(jnp.bfloat16)
    d_mixed = d_mixed.reshape(d_mixed.shape[:-1] + (H, d_mixed.shape[-1] // H))
    d_probs = jnp.einsum(
        layout + "," + key_form + "->bhlm", d_mixed, values, preferred_element_type=jnp.float32
    )
    d_values = jnp.einsum(
        "bhlm," + layout + "->" + key_form, probs_b, d_mixed, preferred_element_type=jnp.float32
    ).astype(jnp.bfloat16)
    centre = jnp.sum(probs * d_probs, axis=-1, keepdims=True)
    d_scores = (probs * (d_probs - centre) * factor).astype(jnp.bfloat16)
    d_queries = jnp.einsum(
        "bhlm," + key_form + "->" + layout, d_scores, key_part, preferred_element_type=jnp.float32
    ).astype(jnp.bfloat16)
    d_keys = jnp.einsum(
        "bhlm," + layout + "->" + key_form, d_scores, queries, preferred_element_type=jnp.float32
    ).astype(jnp.bfloat16)
    joined = jnp.concatenate(
        [merge_heads(d_queries), merge_heads(d_keys), merge_heads(d_values)], axis=-1
    )
    d_normed = jnp.dot(joined, w_in.T, preferred_element_type=jnp.float32)
    scaled = d_normed * gain_vec
    d_tokens = inv_rms * (
        scaled - widened * inv_rms * inv_rms * jnp.mean(scaled * widened, axis=-1, keepdims=True)
    )
    return (upstream.astype(jnp.float32) + d_tokens).astype(jnp.bfloat16)


def line_forward(lines, gain_vec, w_in, w_out):
    feature_count = lines.shape[3]
    flat = lines.reshape(-1, lines.shape[2], feature_count)
    return forward_out(flat, gain_vec, w_in, w_out, "blhe").reshape(lines.shape)


def line_backward(lines, upstream, gain_vec, w_in, w_out):
    feature_count = lines.shape[3]
    flat = lines.reshape(-1, lines.shape[2], feature_count)
    flat_up = upstream.reshape(flat.shape)
    return backward(flat, flat_up, gain_vec, w_in, w_out, "blhe").reshape(lines.shape)


def per_device(tokens, cotangent, gain_x, wqkv_x, wo_x, gain_z, wqkv_z, wo_z):
    full_in_x, full_out_x = (
        lax.all_gather(wqkv_x, "tr", axis=0, tiled=True),
        lax.all_gather(wo_x, "tr", axis=0, tiled=True),
    )
    full_in_z, full_out_z = (
        lax.all_gather(wqkv_z, "tr", axis=0, tiled=True),
        lax.all_gather(wo_z, "tr", axis=0, tiled=True),
    )
    width = tokens.shape[-1]
    lines = lax.all_to_all(tokens, "tr", split_axis=1, concat_axis=2, tiled=True)
    cot_lines = lax.all_to_all(cotangent, "tr", split_axis=1, concat_axis=2, tiled=True)
    cells = lines.shape[1] * lines.shape[2]
    flat = (lines.shape[0], cells, width)
    cot_columns = lax.all_to_all(
        cot_lines.reshape(flat), "gz", split_axis=1, concat_axis=0, tiled=True
    )
    mid_lines = line_forward(lines, gain_x, full_in_x, full_out_x)
    mid_columns = lax.all_to_all(
        mid_lines.reshape(flat), "gz", split_axis=1, concat_axis=0, tiled=True
    )
    grad_columns = backward(
        mid_columns, cot_columns, gain_z, full_in_z, full_out_z, "lbhe"
    )
    grad_lines = lax.all_to_all(grad_columns, "gz", split_axis=0, concat_axis=1, tiled=True)
    result_lines = line_backward(lines, grad_lines.reshape(lines.shape), gain_x, full_in_x, full_out_x)
    return lax.all_to_all(result_lines, "tr", split_axis=2, concat_axis=1, tiled=True)


F32, BF16 = jnp.float32, jnp.bfloat16


def nt(a, b):
    return lax.dot_general(a, b, (((1,), (1,)), ((), ())), preferred_element_type=F32)


def tn(a, b):
    return lax.dot_general(a, b, (((0,), (0,)), ((), ())), preferred_element_type=F32)


def nn(a, b):
    return jnp.dot(a, b, preferred_element_type=F32)


def flat(value):
    width = value.shape[-1]
    return value.astype(F32).reshape(-1, width)


def project(a, gain, w, qkv):
    rows, width = a.shape
    rstd = lax.rsqrt(jnp.mean(a * a, axis=-1, keepdims=True) + 1e-06)
    normed = (a * rstd * gain).astype(BF16)

    def part(j, _):
        cols = pl.ds(pl.multiple_of(j * width, width), width)
        qkv[:, cols] = nn(normed, w[:, cols]).astype(BF16)
        return 0

    lax.fori_loop(0, 3, part, 0)
    return rstd


def line_mask(block, line):
    key = lax.broadcasted_iota(jnp.int32, (block, block), 0) // line
    query = lax.broadcasted_iota(jnp.int32, (block, block), 1) // line
    return key == query


def softmax_of(q, k, mask, factor):
    scores = jnp.where(mask, nt(k, q) * factor, -1e30)
    grown = jnp.exp(scores - jnp.max(scores, axis=0, keepdims=True))
    return grown / jnp.sum(grown, axis=0, keepdims=True)


def attend_forward(qkv, probs, mixed, block, line):
    rows, width = mixed.shape
    size = width // H
    mask = line_mask(block, line)
    factor = 1.0 / math.sqrt(size)

    def body(b, _):
        at = pl.ds(pl.multiple_of(b * block, block), block)
        for h in range(H):
            q, k, v = (qkv[at, n * width + h * size : n * width + (h + 1) * size] for n in range(3))
            p = softmax_of(q, k, mask, factor)
            probs[b * H + h] = p
            mixed[at, h * size : (h + 1) * size] = tn(p.astype(BF16), v).astype(BF16)
        return 0

    lax.fori_loop(0, rows // block, body, 0)


def attend_backward(qkv, probs, d_mixed, joined, block, line, keep):
    rows, width = d_mixed.shape
    size = width // H
    mask = line_mask(block, line)
    factor = 1.0 / math.sqrt(size)

    def body(b, _):
        at = pl.ds(pl.multiple_of(b * block, block), block)
        for h in range(H):
            q, k, v = (qkv[at, n * width + h * size : n * width + (h + 1) * size] for n in range(3))
            p = probs[b * H + h] if keep else softmax_of(q, k, mask, factor)
            dm = d_mixed[at, h * size : (h + 1) * size]
            dp = nt(v, dm)
            dv = nn(p.astype(BF16), dm).astype(BF16)
            centre = jnp.sum(p * dp, axis=0, keepdims=True)
            ds = (p * (dp - centre) * factor).astype(BF16)
            joined[at, h * size : (h + 1) * size] = tn(ds, k).astype(BF16)
            joined[at, width + h * size : width + (h + 1) * size] = nn(ds, q).astype(BF16)
            joined[at, 2 * width + h * size : 2 * width + (h + 1) * size] = dv
        return 0

    lax.fori_loop(0, rows // block, body, 0)


def norm_backward(a, c, rstd, gain, joined, w, dn):
    width = a.shape[-1]
    for j in range(3):
        part = width // 3
        dn[:, j * part : (j + 1) * part] = nt(joined[...], w[j * part : (j + 1) * part, :])
    scaled = dn[...] * gain
    mean = jnp.mean(scaled * a, axis=-1, keepdims=True)
    return (c + rstd * (scaled - a * (rstd * rstd) * mean)).astype(BF16)


def kernel(
    nt_, ng, block_x, line_x, block_z, line_z,
    tok, cot, gain_x, wx, ox, gain_z, wz, oz, px, pz, out,
    tokr, cotr, outs, outr, mids, midr, cots, cotz, grads, gradr,
    fwx, fox, fwz, foz, qkvx, qkvz, probs, mixed, dmix, joined, dn, ax, az,
    tr_send, tr_recv, gz_send, gz_recv, w_send, w_recv, local,
):
    me, mine = lax.axis_index("tr"), lax.axis_index("gz")
    sib, across = me + 1 - 2 * (me % 2), (me + 2) % nt_
    half = mine % 2
    partner = mine + 1 - 2 * half
    rows, width = ax.shape

    barrier = pltpu.get_barrier_semaphore()
    for d in range(1, nt_):
        pl.semaphore_signal(barrier, inc=1, device_id=((me + d) % nt_, mine), device_id_type=pl.DeviceIdType.MESH)
    for d in range(1, ng):
        pl.semaphore_signal(barrier, inc=1, device_id=(me, (mine + d) % ng), device_id_type=pl.DeviceIdType.MESH)
    pl.semaphore_wait(barrier, nt_ + ng - 2)

    def remote(src, dst, send, recv, t, g):
        return pltpu.make_async_remote_copy(
            src_ref=src, dst_ref=dst, send_sem=send, recv_sem=recv,
            device_id=(t, g), device_id_type=pl.DeviceIdType.MESH,
        )

    def tr_copy(n, source, slots, d):
        t = (me + d) % nt_
        return remote(source(t), slots.at[me], tr_send.at[n, d], tr_recv.at[n, d], t, mine)

    def gz_copy(n, source, slots, d):
        g = (mine + d) % ng
        return remote(source.at[g], slots.at[mine], gz_send.at[n, d], gz_recv.at[n, d], me, g)

    far_first = [2, 3, 1] if nt_ == 4 else list(range(1, nt_))
    gz_order = sorted(range(1, ng), key=lambda d: -min(d, ng - d))

    owns = ((wx, ox), (wz, oz))
    fulls = ((fwx, fox), (fwz, foz))

    def piece(ref, t, h, mine_only):
        depth = ref.shape[0] if mine_only else ref.shape[0] // nt_
        cols = ref.shape[1] // 2
        col = pl.ds(pl.multiple_of(h * cols, 128), cols)
        row = pl.ds(0, depth) if mine_only else pl.ds(pl.multiple_of(t * depth, 16), depth)
        return ref.at[row, col]

    def own_copy(s, k, n, h, t):
        return remote(
            piece(owns[s][k], me, h, True), piece(fulls[s][k], me, h, False),
            w_send.at[s, k, n], w_recv.at[s, k, me, h], t, mine,
        )

    def relay(s, k, n, h, t, g):
        spot = piece(fulls[s][k], across, h, False)
        return remote(spot, spot, w_send.at[s, k, n], w_recv.at[s, k, across, h], t, g)

    def arrive(s, k, src, h):
        spot = piece(fulls[s][k], src, h, False)
        remote(spot, spot, w_send.at[s, k, 0], w_recv.at[s, k, src, h], sib, mine).wait_recv()

    def weights_begin(s):
        for k in range(2):
            own_copy(s, k, 2, half, across).start()
        for k in range(2):
            own_copy(s, k, 0, 0, sib).start()
            own_copy(s, k, 1, 1, sib).start()

    def weights_relay(s):
        for k in range(2):
            arrive(s, k, across, half)
            relay(s, k, 3, half, me, partner).start()
            relay(s, k, 4, half, sib, mine).start()

    def weights_end(s):
        far = (sib + 2) % nt_
        for k in range(2):
            arrive(s, k, across, 1 - half)
            relay(s, k, 5, 1 - half, sib, mine).start()
        for k in range(2):
            for h in range(2):
                arrive(s, k, sib, h)
                arrive(s, k, far, h)
            own_copy(s, k, 0, 0, sib).wait_send()
            own_copy(s, k, 1, 1, sib).wait_send()
            own_copy(s, k, 2, half, across).wait_send()
            relay(s, k, 3, half, me, partner).wait_send()
            relay(s, k, 4, half, sib, mine).wait_send()
            relay(s, k, 5, 1 - half, sib, mine).wait_send()

    def wait_tr(n, source, slots):
        for d in range(1, nt_):
            tr_copy(n, source, slots, d).wait_send()
            src = (me + nt_ - d) % nt_
            remote(source(src), slots.at[src], tr_send.at[n, d], tr_recv.at[n, d], src, mine).wait_recv()

    def wait_gz(n, source, slots):
        for d in range(1, ng):
            gz_copy(n, source, slots, d).wait_send()
            src = (mine + ng - d) % ng
            remote(source.at[src], slots.at[src], gz_send.at[n, d], gz_recv.at[n, d], me, src).wait_recv()

    def from_tok(t):
        return tok.at[:, t]

    def from_cot(t):
        return cot.at[:, t]

    def from_out(t):
        return outs.at[t]

    for d in far_first:
        tr_copy(0, from_tok, tokr, d).start()
    weights_begin(0)
    for d in far_first:
        tr_copy(1, from_cot, cotr, d).start()
    here = [pltpu.make_async_copy(tok.at[:, me], tokr.at[me], local.at[0]),
            pltpu.make_async_copy(cot.at[:, me], cotr.at[me], local.at[1])]
    n = 2
    for s in range(2):
        for k in range(2):
            depth = owns[s][k].shape[0]
            to = fulls[s][k].at[pl.ds(pl.multiple_of(me * depth, 16), depth)]
            here.append(pltpu.make_async_copy(owns[s][k], to, local.at[n]))
            n += 1
    for copy in here:
        copy.start()
    for copy in here:
        copy.wait()
    wait_tr(0, from_tok, tokr)
    ax[...] = nn(px[...], flat(tokr[...]).astype(BF16)).astype(BF16)

    weights_relay(0)
    weights_begin(1)
    wait_tr(1, from_cot, cotr)
    cot_lines = nn(px[...], flat(cotr[...]).astype(BF16))
    cots[...] = cot_lines.reshape(cots.shape).astype(BF16)
    cotz[mine] = cots[mine]
    for d in gz_order:
        gz_copy(1, cots, cotz, d).start()
    weights_end(0)

    rstd_x = project(ax[...].astype(F32), gain_x[...], fwx, qkvx)
    attend_forward(qkvx, probs, mixed, block_x, line_x)
    mid = ax[...].astype(F32) + nn(mixed[...], fox[...])
    mids[...] = mid.reshape(mids.shape).astype(BF16)
    for d in gz_order:
        gz_copy(0, mids, midr, d).start()
    midr[mine] = mids[mine]
    weights_relay(1)
    weights_end(1)

    wait_gz(1, cots, cotz)
    cz = nn(pz[...], flat(cotz[...]).astype(BF16))
    dmix[...] = nt(cz.astype(BF16), foz[...]).astype(BF16)
    wait_gz(0, mids, midr)
    az[...] = nn(pz[...], flat(midr[...]).astype(BF16)).astype(BF16)
    rstd_z = project(az[...].astype(F32), gain_z[...], fwz, qkvz)
    attend_backward(qkvz, probs, dmix, joined, block_z, line_z, False)
    cz = nn(pz[...], flat(cotz[...]).astype(BF16))
    back = norm_backward(az[...].astype(F32), cz, rstd_z, gain_z[...], joined, fwz, dn)
    grads[...] = tn(pz[...], back).reshape(grads.shape).astype(BF16)
    for d in gz_order:
        gz_copy(2, grads, gradr, d).start()
    gradr[mine] = grads[mine]
    wait_gz(2, grads, gradr)

    dmix[...] = nt(flat(gradr[...]).astype(BF16), fox[...]).astype(BF16)
    attend_backward(qkvx, probs, dmix, joined, block_x, line_x, True)
    back = norm_backward(
        ax[...].astype(F32), flat(gradr[...]), rstd_x, gain_x[...], joined, fwx, dn
    )
    outs[...] = tn(px[...], back).reshape(outs.shape).astype(BF16)
    for d in far_first:
        tr_copy(2, from_out, outr, d).start()
    outr[me] = outs[me]
    wait_tr(2, from_out, outr)
    for t in range(nt_):
        out[:, t] = outr[t]


def one_hot(order):
    return jnp.asarray(np.eye(len(order), dtype=np.float32)[order], BF16)


def fits_kernel(trs, gzs, slab, y, x_own, width):
    rows_own = y // trs
    return trs == 4 and rows_own == gzs and (slab * trs * x_own) % 8 == 0 and (rows_own * x_own) % 16 == 0


def fused(trs, gzs, tokens, cotangent, gain_x, wqkv_x, wo_x, gain_z, wqkv_z, wo_z):
    slab, y, x_own, width = tokens.shape
    y_own, x = y // trs, x_own * trs
    rows, z = slab * y * x_own, slab * gzs
    share = rows // gzs
    index = np.arange(rows).reshape(trs, slab, y_own, x_own)
    px = one_hot(index.transpose(2, 1, 0, 3).reshape(-1))
    pz = one_hot(np.arange(rows).reshape(z, x).T.reshape(-1))
    split = (slab, trs, y_own * x_own, width)
    block_x, block_z = 80 if 80 % x == 0 else x, 80 if 80 % z == 0 else z
    tr_slots, gz_slots = (trs, slab, y_own * x_own, width), (gzs, share, width)
    vm = pl.BlockSpec(memory_space=pltpu.VMEM)
    hbm = pl.BlockSpec(memory_space=pl.ANY)
    wide = wqkv_x.shape[1]
    result = pl.pallas_call(
        functools.partial(kernel, trs, gzs, block_x, x, block_z, z),
        out_shape=jax.ShapeDtypeStruct(split, BF16),
        in_specs=[hbm, hbm, vm, hbm, hbm, vm, hbm, hbm, vm, vm],
        out_specs=vm,
        scratch_shapes=[pltpu.VMEM(tr_slots, BF16)] * 4
        + [pltpu.VMEM(gz_slots, BF16)] * 6
        + [pltpu.VMEM((width, wide), BF16), pltpu.VMEM((width, width), BF16)] * 2
        + [pltpu.VMEM((rows, wide), BF16)] * 2
        + [pltpu.VMEM((rows // block_x * H, block_x, block_x), F32)]
        + [pltpu.VMEM((rows, width), BF16)] * 2
        + [pltpu.VMEM((rows, wide), BF16), pltpu.VMEM((rows, width), F32)]
        + [pltpu.VMEM((rows, width), BF16)] * 2
        + [
            pltpu.SemaphoreType.DMA((3, trs)),
            pltpu.SemaphoreType.DMA((3, trs)),
            pltpu.SemaphoreType.DMA((3, gzs)),
            pltpu.SemaphoreType.DMA((3, gzs)),
            pltpu.SemaphoreType.DMA((2, 2, 6)),
            pltpu.SemaphoreType.DMA((2, 2, trs, 2)),
            pltpu.SemaphoreType.DMA((6,)),
        ],
        compiler_params=pltpu.CompilerParams(
            collective_id=0, has_side_effects=True, vmem_limit_bytes=56 * 1024 * 1024
        ),
    )(
        tokens.reshape(split), cotangent.reshape(split),
        gain_x.reshape(1, width), wqkv_x, wo_x, gain_z.reshape(1, width), wqkv_z, wo_z, px, pz,
    )
    return result.reshape(tokens.shape)


def solution(mesh):
    trs, gzs = mesh.shape["tr"], mesh.shape["gz"]

    def body(tokens, *rest):
        if fits_kernel(trs, gzs, *tokens.shape):
            return fused(trs, gzs, tokens, *rest)
        return per_device(tokens, *rest)

    return jax.shard_map(
        body,
        mesh=mesh,
        in_specs=(
            P("gz", None, "tr", None),
            P("gz", None, "tr", None),
            P(),
            P("tr", None),
            P("tr", None),
            P(),
            P("tr", None),
            P("tr", None),
        ),
        out_specs=P("gz", None, "tr", None),
        check_vma=False,
    )
```

```python
import functools
import math

import jax
import jax.numpy as jnp
import numpy as np
from jax import lax
from jax.experimental import pallas as pl
from jax.experimental.pallas import tpu as pltpu
from jax.sharding import PartitionSpec as P

H = 6


def head_split(packed, index, model_width):
    piece = packed[..., index * model_width : (index + 1) * model_width]
    return piece.reshape(piece.shape[:-1] + (H, model_width // H))


def merge_heads(value):
    return value.reshape(value.shape[:-2] + (value.shape[-2] * value.shape[-1],))


def recompute(tokens_in, gain_vec, w_in, layout):
    model_width = w_in.shape[0]
    factor = 1.0 / math.sqrt(model_width // H)
    widened = tokens_in.astype(jnp.float32)
    inv_rms = lax.rsqrt(jnp.mean(widened * widened, axis=-1, keepdims=True) + 1e-06)
    normed = (widened * inv_rms * gain_vec).astype(jnp.bfloat16)
    packed = jnp.dot(normed, w_in, preferred_element_type=jnp.float32).astype(jnp.bfloat16)
    queries = head_split(packed, 0, model_width)
    key_part = head_split(packed, 1, model_width)
    values = head_split(packed, 2, model_width)
    key_form = layout.replace("l", "m")
    scores = (
        jnp.einsum(
            layout + "," + key_form + "->bhlm",
            queries,
            key_part,
            preferred_element_type=jnp.float32,
        )
        * factor
    )
    highest = jnp.max(scores, axis=-1, keepdims=True)
    expanded = jnp.exp(scores - highest)
    probs = expanded / jnp.sum(expanded, axis=-1, keepdims=True)
    return (widened, inv_rms, queries, key_part, values, probs, probs.astype(jnp.bfloat16), factor)


def forward_out(tokens_in, gain_vec, w_in, w_out, layout):
    widened, inv_rms, queries, key_part, values, probs, probs_b, factor = recompute(
        tokens_in, gain_vec, w_in, layout
    )
    key_form = layout.replace("l", "m")
    mixed = jnp.einsum(
        "bhlm," + key_form + "->" + layout, probs_b, values, preferred_element_type=jnp.float32
    )
    mixed = merge_heads(mixed.astype(jnp.bfloat16))
    return (widened + jnp.dot(mixed, w_out, preferred_element_type=jnp.float32)).astype(
        jnp.bfloat16
    )


def backward(tokens_in, upstream, gain_vec, w_in, w_out, layout):
    widened, inv_rms, queries, key_part, values, probs, probs_b, factor = recompute(
        tokens_in, gain_vec, w_in, layout
    )
    key_form = layout.replace("l", "m")
    d_mixed = jnp.dot(upstream, w_out.T, preferred_element_type=jnp.float32).astype(jnp.bfloat16)
    d_mixed = d_mixed.reshape(d_mixed.shape[:-1] + (H, d_mixed.shape[-1] // H))
    d_probs = jnp.einsum(
        layout + "," + key_form + "->bhlm", d_mixed, values, preferred_element_type=jnp.float32
    )
    d_values = jnp.einsum(
        "bhlm," + layout + "->" + key_form, probs_b, d_mixed, preferred_element_type=jnp.float32
    ).astype(jnp.bfloat16)
    centre = jnp.sum(probs * d_probs, axis=-1, keepdims=True)
    d_scores = (probs * (d_probs - centre) * factor).astype(jnp.bfloat16)
    d_queries = jnp.einsum(
        "bhlm," + key_form + "->" + layout, d_scores, key_part, preferred_element_type=jnp.float32
    ).astype(jnp.bfloat16)
    d_keys = jnp.einsum(
        "bhlm," + layout + "->" + key_form, d_scores, queries, preferred_element_type=jnp.float32
    ).astype(jnp.bfloat16)
    joined = jnp.concatenate(
        [merge_heads(d_queries), merge_heads(d_keys), merge_heads(d_values)], axis=-1
    )
    d_normed = jnp.dot(joined, w_in.T, preferred_element_type=jnp.float32)
    scaled = d_normed * gain_vec
    d_tokens = inv_rms * (
        scaled - widened * inv_rms * inv_rms * jnp.mean(scaled * widened, axis=-1, keepdims=True)
    )
    return (upstream.astype(jnp.float32) + d_tokens).astype(jnp.bfloat16)


def line_forward(lines, gain_vec, w_in, w_out):
    feature_count = lines.shape[3]
    flat = lines.reshape(-1, lines.shape[2], feature_count)
    return forward_out(flat, gain_vec, w_in, w_out, "blhe").reshape(lines.shape)


def line_backward(lines, upstream, gain_vec, w_in, w_out):
    feature_count = lines.shape[3]
    flat = lines.reshape(-1, lines.shape[2], feature_count)
    flat_up = upstream.reshape(flat.shape)
    return backward(flat, flat_up, gain_vec, w_in, w_out, "blhe").reshape(lines.shape)


def per_device(tokens, cotangent, gain_x, wqkv_x, wo_x, gain_z, wqkv_z, wo_z):
    full_in_x, full_out_x = (
        lax.all_gather(wqkv_x, "tr", axis=0, tiled=True),
        lax.all_gather(wo_x, "tr", axis=0, tiled=True),
    )
    full_in_z, full_out_z = (
        lax.all_gather(wqkv_z, "tr", axis=0, tiled=True),
        lax.all_gather(wo_z, "tr", axis=0, tiled=True),
    )
    width = tokens.shape[-1]
    lines = lax.all_to_all(tokens, "tr", split_axis=1, concat_axis=2, tiled=True)
    cot_lines = lax.all_to_all(cotangent, "tr", split_axis=1, concat_axis=2, tiled=True)
    cells = lines.shape[1] * lines.shape[2]
    flat = (lines.shape[0], cells, width)
    cot_columns = lax.all_to_all(
        cot_lines.reshape(flat), "gz", split_axis=1, concat_axis=0, tiled=True
    )
    mid_lines = line_forward(lines, gain_x, full_in_x, full_out_x)
    mid_columns = lax.all_to_all(
        mid_lines.reshape(flat), "gz", split_axis=1, concat_axis=0, tiled=True
    )
    grad_columns = backward(
        mid_columns, cot_columns, gain_z, full_in_z, full_out_z, "lbhe"
    )
    grad_lines = lax.all_to_all(grad_columns, "gz", split_axis=0, concat_axis=1, tiled=True)
    result_lines = line_backward(lines, grad_lines.reshape(lines.shape), gain_x, full_in_x, full_out_x)
    return lax.all_to_all(result_lines, "tr", split_axis=2, concat_axis=1, tiled=True)


F32, BF16 = jnp.float32, jnp.bfloat16


def nt(a, b):
    return lax.dot_general(a, b, (((1,), (1,)), ((), ())), preferred_element_type=F32)


def tn(a, b):
    return lax.dot_general(a, b, (((0,), (0,)), ((), ())), preferred_element_type=F32)


def nn(a, b):
    return jnp.dot(a, b, preferred_element_type=F32)


def flat(value):
    width = value.shape[-1]
    return value.astype(F32).reshape(-1, width)


def project(a, gain, w, qkv):
    rows, width = a.shape
    rstd = lax.rsqrt(jnp.mean(a * a, axis=-1, keepdims=True) + 1e-06)
    normed = (a * rstd * gain).astype(BF16)

    def part(j, _):
        cols = pl.ds(pl.multiple_of(j * width, width), width)
        qkv[:, cols] = nn(normed, w[:, cols]).astype(BF16)
        return 0

    lax.fori_loop(0, 3, part, 0)
    return rstd


def line_mask(block, line):
    key = lax.broadcasted_iota(jnp.int32, (block, block), 0) // line
    query = lax.broadcasted_iota(jnp.int32, (block, block), 1) // line
    return key == query


def softmax_of(q, k, mask, factor):
    scores = jnp.where(mask, nt(k, q) * factor, -1e30)
    grown = jnp.exp(scores - jnp.max(scores, axis=0, keepdims=True))
    return grown / jnp.sum(grown, axis=0, keepdims=True)


def attend_forward(qkv, probs, mixed, block, line):
    rows, width = mixed.shape
    size = width // H
    mask = line_mask(block, line)
    factor = 1.0 / math.sqrt(size)

    def body(b, _):
        at = pl.ds(pl.multiple_of(b * block, block), block)
        for h in range(H):
            q, k, v = (qkv[at, n * width + h * size : n * width + (h + 1) * size] for n in range(3))
            p = softmax_of(q, k, mask, factor)
            probs[b * H + h] = p
            mixed[at, h * size : (h + 1) * size] = tn(p.astype(BF16), v).astype(BF16)
        return 0

    lax.fori_loop(0, rows // block, body, 0)


def attend_backward(qkv, probs, d_mixed, joined, block, line, keep):
    rows, width = d_mixed.shape
    size = width // H
    mask = line_mask(block, line)
    factor = 1.0 / math.sqrt(size)

    def body(b, _):
        at = pl.ds(pl.multiple_of(b * block, block), block)
        for h in range(H):
            q, k, v = (qkv[at, n * width + h * size : n * width + (h + 1) * size] for n in range(3))
            p = probs[b * H + h] if keep else softmax_of(q, k, mask, factor)
            dm = d_mixed[at, h * size : (h + 1) * size]
            dp = nt(v, dm)
            dv = nn(p.astype(BF16), dm).astype(BF16)
            centre = jnp.sum(p * dp, axis=0, keepdims=True)
            ds = (p * (dp - centre) * factor).astype(BF16)
            joined[at, h * size : (h + 1) * size] = tn(ds, k).astype(BF16)
            joined[at, width + h * size : width + (h + 1) * size] = nn(ds, q).astype(BF16)
            joined[at, 2 * width + h * size : 2 * width + (h + 1) * size] = dv
        return 0

    lax.fori_loop(0, rows // block, body, 0)


def norm_backward(a, c, rstd, gain, joined, w, dn):
    width = a.shape[-1]
    for j in range(3):
        part = width // 3
        dn[:, j * part : (j + 1) * part] = nt(joined[...], w[j * part : (j + 1) * part, :])
    scaled = dn[...] * gain
    mean = jnp.mean(scaled * a, axis=-1, keepdims=True)
    return (c + rstd * (scaled - a * (rstd * rstd) * mean)).astype(BF16)


def kernel(
    nt_, ng, block_x, line_x, block_z, line_z,
    tok, cot, gain_x, wx, ox, gain_z, wz, oz, px, pz, out,
    tokr, cotr, outs, outr, mids, midr, cots, cotz, grads, gradr,
    fwx, fox, fwz, foz, qkvx, qkvz, probs, mixed, dmix, joined, dn, ax, az,
    tr_send, tr_recv, gz_send, gz_recv, w_send, w_recv, local,
):
    me, mine = lax.axis_index("tr"), lax.axis_index("gz")
    sib, across = me + 1 - 2 * (me % 2), (me + 2) % nt_
    half = mine % 2
    partner = mine + 1 - 2 * half
    rows, width = ax.shape

    barrier = pltpu.get_barrier_semaphore()
    for d in range(1, nt_):
        pl.semaphore_signal(barrier, inc=1, device_id=((me + d) % nt_, mine), device_id_type=pl.DeviceIdType.MESH)
    for d in range(1, ng):
        pl.semaphore_signal(barrier, inc=1, device_id=(me, (mine + d) % ng), device_id_type=pl.DeviceIdType.MESH)
    pl.semaphore_wait(barrier, nt_ + ng - 2)

    def remote(src, dst, send, recv, t, g):
        return pltpu.make_async_remote_copy(
            src_ref=src, dst_ref=dst, send_sem=send, recv_sem=recv,
            device_id=(t, g), device_id_type=pl.DeviceIdType.MESH,
        )

    def tr_copy(n, source, slots, d):
        t = (me + d) % nt_
        return remote(source(t), slots.at[me], tr_send.at[n, d], tr_recv.at[n, d], t, mine)

    def gz_copy(n, source, slots, d):
        g = (mine + d) % ng
        return remote(source.at[g], slots.at[mine], gz_send.at[n, d], gz_recv.at[n, d], me, g)

    far_first = [2, 3, 1] if nt_ == 4 else list(range(1, nt_))
    gz_order = sorted(range(1, ng), key=lambda d: -min(d, ng - d))

    owns = ((wx, wx, wx, ox), (wz, wz, wz, oz))
    fulls = ((fwx, fwx, fwx, fox), (fwz, fwz, fwz, foz))

    def piece(ref, k, t, h, mine_only):
        depth = ref.shape[0] if mine_only else ref.shape[0] // nt_
        cols = width // 2
        first = h * 3 + k if k < 3 else h
        col = pl.ds(pl.multiple_of(first * cols, 128), cols)
        row = pl.ds(0, depth) if mine_only else pl.ds(pl.multiple_of(t * depth, 16), depth)
        return ref.at[row, col]

    def own_copy(s, k, n, h, t):
        return remote(
            piece(owns[s][k], k, me, h, True), piece(fulls[s][k], k, me, h, False),
            w_send.at[s, k, n], w_recv.at[s, k, me, h], t, mine,
        )

    def relay(s, k, n, h, t, g):
        spot = piece(fulls[s][k], k, across, h, False)
        return remote(spot, spot, w_send.at[s, k, n], w_recv.at[s, k, across, h], t, g)

    def arrive(s, k, src, h):
        spot = piece(fulls[s][k], k, src, h, False)
        remote(spot, spot, w_send.at[s, k, 0], w_recv.at[s, k, src, h], sib, mine).wait_recv()

    def weights_begin(s):
        for k in range(4):
            own_copy(s, k, 2, half, across).start()
        for k in range(4):
            own_copy(s, k, 0, 0, sib).start()
            own_copy(s, k, 1, 1, sib).start()

    def weights_relay(s):
        for k in range(4):
            arrive(s, k, across, half)
            relay(s, k, 3, half, me, partner).start()
            relay(s, k, 4, half, sib, mine).start()

    def weights_end(s):
        far = (sib + 2) % nt_
        for k in range(4):
            arrive(s, k, across, 1 - half)
            relay(s, k, 5, 1 - half, sib, mine).start()
        for k in range(4):
            for h in range(2):
                arrive(s, k, sib, h)
                arrive(s, k, far, h)
            own_copy(s, k, 0, 0, sib).wait_send()
            own_copy(s, k, 1, 1, sib).wait_send()
            own_copy(s, k, 2, half, across).wait_send()
            relay(s, k, 3, half, me, partner).wait_send()
            relay(s, k, 4, half, sib, mine).wait_send()
            relay(s, k, 5, 1 - half, sib, mine).wait_send()

    def wait_tr(n, source, slots):
        for d in range(1, nt_):
            tr_copy(n, source, slots, d).wait_send()
            src = (me + nt_ - d) % nt_
            remote(source(src), slots.at[src], tr_send.at[n, d], tr_recv.at[n, d], src, mine).wait_recv()

    def wait_gz(n, source, slots):
        for d in range(1, ng):
            gz_copy(n, source, slots, d).wait_send()
            src = (mine + ng - d) % ng
            remote(source.at[src], slots.at[src], gz_send.at[n, d], gz_recv.at[n, d], me, src).wait_recv()

    def from_tok(t):
        return tok.at[:, t]

    def from_cot(t):
        return cot.at[:, t]

    def from_out(t):
        return outs.at[t]

    for d in far_first:
        tr_copy(0, from_tok, tokr, d).start()
    weights_begin(0)
    for d in far_first:
        tr_copy(1, from_cot, cotr, d).start()
    here = [pltpu.make_async_copy(tok.at[:, me], tokr.at[me], local.at[0]),
            pltpu.make_async_copy(cot.at[:, me], cotr.at[me], local.at[1])]
    n = 2
    for s in range(2):
        for k in (0, 3):
            depth = owns[s][k].shape[0]
            to = fulls[s][k].at[pl.ds(pl.multiple_of(me * depth, 16), depth)]
            here.append(pltpu.make_async_copy(owns[s][k], to, local.at[n]))
            n += 1
    for copy in here:
        copy.start()
    for copy in here:
        copy.wait()
    wait_tr(0, from_tok, tokr)
    ax[...] = nn(px[...], flat(tokr[...]).astype(BF16)).astype(BF16)

    weights_relay(0)
    weights_begin(1)
    wait_tr(1, from_cot, cotr)
    cot_lines = nn(px[...], flat(cotr[...]).astype(BF16))
    cots[...] = cot_lines.reshape(cots.shape).astype(BF16)
    cotz[mine] = cots[mine]
    for d in gz_order:
        gz_copy(1, cots, cotz, d).start()
    weights_end(0)

    rstd_x = project(ax[...].astype(F32), gain_x[...], fwx, qkvx)
    attend_forward(qkvx, probs, mixed, block_x, line_x)
    mid = ax[...].astype(F32) + nn(mixed[...], fox[...])
    mids[...] = mid.reshape(mids.shape).astype(BF16)
    for d in gz_order:
        gz_copy(0, mids, midr, d).start()
    midr[mine] = mids[mine]
    weights_relay(1)
    weights_end(1)

    wait_gz(1, cots, cotz)
    cz = nn(pz[...], flat(cotz[...]).astype(BF16))
    dmix[...] = nt(cz.astype(BF16), foz[...]).astype(BF16)
    wait_gz(0, mids, midr)
    az[...] = nn(pz[...], flat(midr[...]).astype(BF16)).astype(BF16)
    rstd_z = project(az[...].astype(F32), gain_z[...], fwz, qkvz)
    attend_backward(qkvz, probs, dmix, joined, block_z, line_z, False)
    cz = nn(pz[...], flat(cotz[...]).astype(BF16))
    back = norm_backward(az[...].astype(F32), cz, rstd_z, gain_z[...], joined, fwz, dn)
    grads[...] = tn(pz[...], back).reshape(grads.shape).astype(BF16)
    for d in gz_order:
        gz_copy(2, grads, gradr, d).start()
    gradr[mine] = grads[mine]
    wait_gz(2, grads, gradr)

    dmix[...] = nt(flat(gradr[...]).astype(BF16), fox[...]).astype(BF16)
    attend_backward(qkvx, probs, dmix, joined, block_x, line_x, True)
    back = norm_backward(
        ax[...].astype(F32), flat(gradr[...]), rstd_x, gain_x[...], joined, fwx, dn
    )
    outs[...] = tn(px[...], back).reshape(outs.shape).astype(BF16)
    for d in far_first:
        tr_copy(2, from_out, outr, d).start()
    outr[me] = outs[me]
    wait_tr(2, from_out, outr)
    for t in range(nt_):
        out[:, t] = outr[t]


def one_hot(order):
    return jnp.asarray(np.eye(len(order), dtype=np.float32)[order], BF16)


def fits_kernel(trs, gzs, slab, y, x_own, width):
    rows_own = y // trs
    return trs == 4 and rows_own == gzs and (slab * trs * x_own) % 8 == 0 and (rows_own * x_own) % 16 == 0


def fused(trs, gzs, tokens, cotangent, gain_x, wqkv_x, wo_x, gain_z, wqkv_z, wo_z):
    slab, y, x_own, width = tokens.shape
    y_own, x = y // trs, x_own * trs
    rows, z = slab * y * x_own, slab * gzs
    share = rows // gzs
    index = np.arange(rows).reshape(trs, slab, y_own, x_own)
    px = one_hot(index.transpose(2, 1, 0, 3).reshape(-1))
    pz = one_hot(np.arange(rows).reshape(z, x).T.reshape(-1))
    split = (slab, trs, y_own * x_own, width)
    block_x, block_z = 80 if 80 % x == 0 else x, 80 if 80 % z == 0 else z
    tr_slots, gz_slots = (trs, slab, y_own * x_own, width), (gzs, share, width)
    vm = pl.BlockSpec(memory_space=pltpu.VMEM)
    hbm = pl.BlockSpec(memory_space=pl.ANY)
    wide = wqkv_x.shape[1]
    result = pl.pallas_call(
        functools.partial(kernel, trs, gzs, block_x, x, block_z, z),
        out_shape=jax.ShapeDtypeStruct(split, BF16),
        in_specs=[hbm, hbm, vm, hbm, hbm, vm, hbm, hbm, vm, vm],
        out_specs=vm,
        scratch_shapes=[pltpu.VMEM(tr_slots, BF16)] * 4
        + [pltpu.VMEM(gz_slots, BF16)] * 6
        + [pltpu.VMEM((width, wide), BF16), pltpu.VMEM((width, width), BF16)] * 2
        + [pltpu.VMEM((rows, wide), BF16)] * 2
        + [pltpu.VMEM((rows // block_x * H, block_x, block_x), F32)]
        + [pltpu.VMEM((rows, width), BF16)] * 2
        + [pltpu.VMEM((rows, wide), BF16), pltpu.VMEM((rows, width), F32)]
        + [pltpu.VMEM((rows, width), BF16)] * 2
        + [
            pltpu.SemaphoreType.DMA((3, trs)),
            pltpu.SemaphoreType.DMA((3, trs)),
            pltpu.SemaphoreType.DMA((3, gzs)),
            pltpu.SemaphoreType.DMA((3, gzs)),
            pltpu.SemaphoreType.DMA((2, 4, 6)),
            pltpu.SemaphoreType.DMA((2, 4, trs, 2)),
            pltpu.SemaphoreType.DMA((6,)),
        ],
        compiler_params=pltpu.CompilerParams(
            collective_id=0, has_side_effects=True, vmem_limit_bytes=56 * 1024 * 1024
        ),
    )(
        tokens.reshape(split), cotangent.reshape(split),
        gain_x.reshape(1, width), wqkv_x, wo_x, gain_z.reshape(1, width), wqkv_z, wo_z, px, pz,
    )
    return result.reshape(tokens.shape)


def solution(mesh):
    trs, gzs = mesh.shape["tr"], mesh.shape["gz"]

    def body(tokens, *rest):
        if fits_kernel(trs, gzs, *tokens.shape):
            return fused(trs, gzs, tokens, *rest)
        return per_device(tokens, *rest)

    return jax.shard_map(
        body,
        mesh=mesh,
        in_specs=(
            P("gz", None, "tr", None),
            P("gz", None, "tr", None),
            P(),
            P("tr", None),
            P("tr", None),
            P(),
            P("tr", None),
            P("tr", None),
        ),
        out_specs=P("gz", None, "tr", None),
        check_vma=False,
    )
```

```python
import functools
import math

import jax
import jax.numpy as jnp
import numpy as np
from jax import lax
from jax.experimental import pallas as pl
from jax.experimental.pallas import tpu as pltpu
from jax.sharding import PartitionSpec as P

H = 6


def head_split(packed, index, model_width):
    piece = packed[..., index * model_width : (index + 1) * model_width]
    return piece.reshape(piece.shape[:-1] + (H, model_width // H))


def merge_heads(value):
    return value.reshape(value.shape[:-2] + (value.shape[-2] * value.shape[-1],))


def recompute(tokens_in, gain_vec, w_in, layout):
    model_width = w_in.shape[0]
    factor = 1.0 / math.sqrt(model_width // H)
    widened = tokens_in.astype(jnp.float32)
    inv_rms = lax.rsqrt(jnp.mean(widened * widened, axis=-1, keepdims=True) + 1e-06)
    normed = (widened * inv_rms * gain_vec).astype(jnp.bfloat16)
    packed = jnp.dot(normed, w_in, preferred_element_type=jnp.float32).astype(jnp.bfloat16)
    queries = head_split(packed, 0, model_width)
    key_part = head_split(packed, 1, model_width)
    values = head_split(packed, 2, model_width)
    key_form = layout.replace("l", "m")
    scores = (
        jnp.einsum(
            layout + "," + key_form + "->bhlm",
            queries,
            key_part,
            preferred_element_type=jnp.float32,
        )
        * factor
    )
    highest = jnp.max(scores, axis=-1, keepdims=True)
    expanded = jnp.exp(scores - highest)
    probs = expanded / jnp.sum(expanded, axis=-1, keepdims=True)
    return (widened, inv_rms, queries, key_part, values, probs, probs.astype(jnp.bfloat16), factor)


def forward_out(tokens_in, gain_vec, w_in, w_out, layout):
    widened, inv_rms, queries, key_part, values, probs, probs_b, factor = recompute(
        tokens_in, gain_vec, w_in, layout
    )
    key_form = layout.replace("l", "m")
    mixed = jnp.einsum(
        "bhlm," + key_form + "->" + layout, probs_b, values, preferred_element_type=jnp.float32
    )
    mixed = merge_heads(mixed.astype(jnp.bfloat16))
    return (widened + jnp.dot(mixed, w_out, preferred_element_type=jnp.float32)).astype(
        jnp.bfloat16
    )


def backward(tokens_in, upstream, gain_vec, w_in, w_out, layout):
    widened, inv_rms, queries, key_part, values, probs, probs_b, factor = recompute(
        tokens_in, gain_vec, w_in, layout
    )
    key_form = layout.replace("l", "m")
    d_mixed = jnp.dot(upstream, w_out.T, preferred_element_type=jnp.float32).astype(jnp.bfloat16)
    d_mixed = d_mixed.reshape(d_mixed.shape[:-1] + (H, d_mixed.shape[-1] // H))
    d_probs = jnp.einsum(
        layout + "," + key_form + "->bhlm", d_mixed, values, preferred_element_type=jnp.float32
    )
    d_values = jnp.einsum(
        "bhlm," + layout + "->" + key_form, probs_b, d_mixed, preferred_element_type=jnp.float32
    ).astype(jnp.bfloat16)
    centre = jnp.sum(probs * d_probs, axis=-1, keepdims=True)
    d_scores = (probs * (d_probs - centre) * factor).astype(jnp.bfloat16)
    d_queries = jnp.einsum(
        "bhlm," + key_form + "->" + layout, d_scores, key_part, preferred_element_type=jnp.float32
    ).astype(jnp.bfloat16)
    d_keys = jnp.einsum(
        "bhlm," + layout + "->" + key_form, d_scores, queries, preferred_element_type=jnp.float32
    ).astype(jnp.bfloat16)
    joined = jnp.concatenate(
        [merge_heads(d_queries), merge_heads(d_keys), merge_heads(d_values)], axis=-1
    )
    d_normed = jnp.dot(joined, w_in.T, preferred_element_type=jnp.float32)
    scaled = d_normed * gain_vec
    d_tokens = inv_rms * (
        scaled - widened * inv_rms * inv_rms * jnp.mean(scaled * widened, axis=-1, keepdims=True)
    )
    return (upstream.astype(jnp.float32) + d_tokens).astype(jnp.bfloat16)


def line_forward(lines, gain_vec, w_in, w_out):
    feature_count = lines.shape[3]
    flat = lines.reshape(-1, lines.shape[2], feature_count)
    return forward_out(flat, gain_vec, w_in, w_out, "blhe").reshape(lines.shape)


def line_backward(lines, upstream, gain_vec, w_in, w_out):
    feature_count = lines.shape[3]
    flat = lines.reshape(-1, lines.shape[2], feature_count)
    flat_up = upstream.reshape(flat.shape)
    return backward(flat, flat_up, gain_vec, w_in, w_out, "blhe").reshape(lines.shape)


def per_device(tokens, cotangent, gain_x, wqkv_x, wo_x, gain_z, wqkv_z, wo_z):
    full_in_x, full_out_x = (
        lax.all_gather(wqkv_x, "tr", axis=0, tiled=True),
        lax.all_gather(wo_x, "tr", axis=0, tiled=True),
    )
    full_in_z, full_out_z = (
        lax.all_gather(wqkv_z, "tr", axis=0, tiled=True),
        lax.all_gather(wo_z, "tr", axis=0, tiled=True),
    )
    width = tokens.shape[-1]
    lines = lax.all_to_all(tokens, "tr", split_axis=1, concat_axis=2, tiled=True)
    cot_lines = lax.all_to_all(cotangent, "tr", split_axis=1, concat_axis=2, tiled=True)
    cells = lines.shape[1] * lines.shape[2]
    flat = (lines.shape[0], cells, width)
    cot_columns = lax.all_to_all(
        cot_lines.reshape(flat), "gz", split_axis=1, concat_axis=0, tiled=True
    )
    mid_lines = line_forward(lines, gain_x, full_in_x, full_out_x)
    mid_columns = lax.all_to_all(
        mid_lines.reshape(flat), "gz", split_axis=1, concat_axis=0, tiled=True
    )
    grad_columns = backward(
        mid_columns, cot_columns, gain_z, full_in_z, full_out_z, "lbhe"
    )
    grad_lines = lax.all_to_all(grad_columns, "gz", split_axis=0, concat_axis=1, tiled=True)
    result_lines = line_backward(lines, grad_lines.reshape(lines.shape), gain_x, full_in_x, full_out_x)
    return lax.all_to_all(result_lines, "tr", split_axis=2, concat_axis=1, tiled=True)


F32, BF16 = jnp.float32, jnp.bfloat16


def nt(a, b):
    return lax.dot_general(a, b, (((1,), (1,)), ((), ())), preferred_element_type=F32)


def tn(a, b):
    return lax.dot_general(a, b, (((0,), (0,)), ((), ())), preferred_element_type=F32)


def nn(a, b):
    return jnp.dot(a, b, preferred_element_type=F32)


def flat(value):
    width = value.shape[-1]
    return value.astype(F32).reshape(-1, width)


def project(a, gain, w, qkv):
    rows, width = a.shape
    rstd = lax.rsqrt(jnp.mean(a * a, axis=-1, keepdims=True) + 1e-06)
    normed = (a * rstd * gain).astype(BF16)

    def part(j, _):
        cols = pl.ds(pl.multiple_of(j * width, width), width)
        qkv[:, cols] = nn(normed, w[:, cols]).astype(BF16)
        return 0

    lax.fori_loop(0, 3, part, 0)
    return rstd


def line_mask(block, line):
    key = lax.broadcasted_iota(jnp.int32, (block, block), 0) // line
    query = lax.broadcasted_iota(jnp.int32, (block, block), 1) // line
    return key == query


def attend_forward(qkv, probs, mixed, block, line):
    rows, width = mixed.shape
    size = width // H
    mask = line_mask(block, line)
    factor = 1.0 / math.sqrt(size)

    def body(b, _):
        at = pl.ds(pl.multiple_of(b * block, block), block)
        for first in range(0, H, 6):
            heads = range(first, first + 6)
            spans = [[pl.ds(n * width + h * size, size) for n in range(3)] for h in heads]
            qk = [nt(qkv[at, sp[1]], qkv[at, sp[0]]) for sp in spans]
            scores = [jnp.where(mask, x * factor, -1e30) for x in qk]
            tops = [jnp.max(x, axis=0, keepdims=True) for x in scores]
            grown = [jnp.exp(x - t) for x, t in zip(scores, tops)]
            sums = [jnp.sum(x, axis=0, keepdims=True) for x in grown]
            ps = [x / t for x, t in zip(grown, sums)]
            for h, p in zip(heads, ps):
                probs[b * H + h] = p
            outs = [tn(p.astype(BF16), qkv[at, sp[2]]) for p, sp in zip(ps, spans)]
            for sp, o in zip(spans, outs):
                mixed[at, sp[0]] = o.astype(BF16)
        return 0

    lax.fori_loop(0, rows // block, body, 0)


def attend_backward(qkv, probs, d_mixed, joined, block, line, keep):
    rows, width = d_mixed.shape
    size = width // H
    mask = line_mask(block, line)
    factor = 1.0 / math.sqrt(size)

    def body(b, _):
        at = pl.ds(pl.multiple_of(b * block, block), block)
        for first in range(0, H, 6):
            heads = range(first, first + 6)
            spans = [[pl.ds(n * width + h * size, size) for n in range(3)] for h in heads]
            dps = [nt(qkv[at, sp[2]], d_mixed[at, sp[0]]) for sp in spans]
            if keep:
                ps = [probs[b * H + h] for h in heads]
            else:
                qk = [nt(qkv[at, sp[1]], qkv[at, sp[0]]) for sp in spans]
                scores = [jnp.where(mask, x * factor, -1e30) for x in qk]
                tops = [jnp.max(x, axis=0, keepdims=True) for x in scores]
                grown = [jnp.exp(x - t) for x, t in zip(scores, tops)]
                sums = [jnp.sum(x, axis=0, keepdims=True) for x in grown]
                ps = [x / t for x, t in zip(grown, sums)]
            dvs = [nn(p.astype(BF16), d_mixed[at, sp[0]]) for p, sp in zip(ps, spans)]
            centres = [jnp.sum(p * dp, axis=0, keepdims=True) for p, dp in zip(ps, dps)]
            dss = [
                (p * (dp - c) * factor).astype(BF16) for p, dp, c in zip(ps, dps, centres)
            ]
            dks = [nn(ds, qkv[at, sp[0]]) for ds, sp in zip(dss, spans)]
            dqs = [tn(ds, qkv[at, sp[1]]) for ds, sp in zip(dss, spans)]
            for sp, dq, dk, dv in zip(spans, dqs, dks, dvs):
                joined[at, sp[0]] = dq.astype(BF16)
                joined[at, sp[1]] = dk.astype(BF16)
                joined[at, sp[2]] = dv.astype(BF16)
        return 0

    lax.fori_loop(0, rows // block, body, 0)


def norm_backward(a, c, rstd, gain, joined, w, dn):
    width = a.shape[-1]
    for j in range(3):
        part = width // 3
        dn[:, j * part : (j + 1) * part] = nt(joined[...], w[j * part : (j + 1) * part, :])
    scaled = dn[...] * gain
    mean = jnp.mean(scaled * a, axis=-1, keepdims=True)
    return (c + rstd * (scaled - a * (rstd * rstd) * mean)).astype(BF16)


def kernel(
    nt_, ng, block_x, line_x, block_z, line_z,
    tok, cot, gain_x, wx, ox, gain_z, wz, oz, px, pz, out,
    tokr, cotr, outs, outr, mids, midr, cots, cotz, grads, gradr,
    fwx, fox, fwz, foz, qkvx, qkvz, probs, mixed, dmix, joined, dn, ax, az,
    tr_send, tr_recv, gz_send, gz_recv, w_send, w_recv, local,
):
    me, mine = lax.axis_index("tr"), lax.axis_index("gz")
    sib, across = me + 1 - 2 * (me % 2), (me + 2) % nt_
    half = mine % 2
    partner = mine + 1 - 2 * half
    rows, width = ax.shape

    barrier = pltpu.get_barrier_semaphore()
    for d in range(1, nt_):
        pl.semaphore_signal(barrier, inc=1, device_id=((me + d) % nt_, mine), device_id_type=pl.DeviceIdType.MESH)
    for d in range(1, ng):
        pl.semaphore_signal(barrier, inc=1, device_id=(me, (mine + d) % ng), device_id_type=pl.DeviceIdType.MESH)
    pl.semaphore_wait(barrier, nt_ + ng - 2)

    def remote(src, dst, send, recv, t, g):
        return pltpu.make_async_remote_copy(
            src_ref=src, dst_ref=dst, send_sem=send, recv_sem=recv,
            device_id=(t, g), device_id_type=pl.DeviceIdType.MESH,
        )

    def tr_copy(n, source, slots, d):
        t = (me + d) % nt_
        return remote(source(t), slots.at[me], tr_send.at[n, d], tr_recv.at[n, d], t, mine)

    def gz_copy(n, source, slots, d):
        g = (mine + d) % ng
        return remote(source.at[g], slots.at[mine], gz_send.at[n, d], gz_recv.at[n, d], me, g)

    far_first = [2, 3, 1] if nt_ == 4 else list(range(1, nt_))
    gz_order = sorted(range(1, ng), key=lambda d: -min(d, ng - d))

    owns = ((wx, wx, wx, ox), (wz, wz, wz, oz))
    fulls = ((fwx, fwx, fwx, fox), (fwz, fwz, fwz, foz))

    def piece(ref, k, t, h, mine_only):
        depth = ref.shape[0] if mine_only else ref.shape[0] // nt_
        cols = width // 2
        first = h * 3 + k if k < 3 else h
        col = pl.ds(pl.multiple_of(first * cols, 128), cols)
        row = pl.ds(0, depth) if mine_only else pl.ds(pl.multiple_of(t * depth, 16), depth)
        return ref.at[row, col]

    def own_copy(s, k, n, h, t):
        return remote(
            piece(owns[s][k], k, me, h, True), piece(fulls[s][k], k, me, h, False),
            w_send.at[s, k, n], w_recv.at[s, k, me, h], t, mine,
        )

    def relay(s, k, n, h, t, g):
        spot = piece(fulls[s][k], k, across, h, False)
        return remote(spot, spot, w_send.at[s, k, n], w_recv.at[s, k, across, h], t, g)

    def arrive(s, k, src, h):
        spot = piece(fulls[s][k], k, src, h, False)
        remote(spot, spot, w_send.at[s, k, 0], w_recv.at[s, k, src, h], sib, mine).wait_recv()

    def weights_begin(s):
        for k in range(4):
            own_copy(s, k, 2, half, across).start()
        for k in range(4):
            own_copy(s, k, 0, 0, sib).start()
            own_copy(s, k, 1, 1, sib).start()

    def weights_relay(s, pieces=range(4)):
        for k in pieces:
            arrive(s, k, across, half)
            relay(s, k, 3, half, me, partner).start()
            relay(s, k, 4, half, sib, mine).start()

    def weights_end(s):
        far = (sib + 2) % nt_
        for k in range(4):
            arrive(s, k, across, 1 - half)
            relay(s, k, 5, 1 - half, sib, mine).start()
        for k in range(4):
            for h in range(2):
                arrive(s, k, sib, h)
                arrive(s, k, far, h)
            own_copy(s, k, 0, 0, sib).wait_send()
            own_copy(s, k, 1, 1, sib).wait_send()
            own_copy(s, k, 2, half, across).wait_send()
            relay(s, k, 3, half, me, partner).wait_send()
            relay(s, k, 4, half, sib, mine).wait_send()
            relay(s, k, 5, 1 - half, sib, mine).wait_send()

    def wait_tr(n, source, slots):
        for d in range(1, nt_):
            tr_copy(n, source, slots, d).wait_send()
            src = (me + nt_ - d) % nt_
            remote(source(src), slots.at[src], tr_send.at[n, d], tr_recv.at[n, d], src, mine).wait_recv()

    def wait_gz(n, source, slots):
        for d in range(1, ng):
            gz_copy(n, source, slots, d).wait_send()
            src = (mine + ng - d) % ng
            remote(source.at[src], slots.at[src], gz_send.at[n, d], gz_recv.at[n, d], me, src).wait_recv()

    def from_tok(t):
        return tok.at[:, t]

    def from_cot(t):
        return cot.at[:, t]

    def from_out(t):
        return outs.at[t]

    for d in far_first:
        tr_copy(0, from_tok, tokr, d).start()
    weights_begin(0)
    for d in far_first:
        tr_copy(1, from_cot, cotr, d).start()
    here = [pltpu.make_async_copy(tok.at[:, me], tokr.at[me], local.at[0]),
            pltpu.make_async_copy(cot.at[:, me], cotr.at[me], local.at[1])]
    n = 2
    for s in range(2):
        for k in (0, 3):
            depth = owns[s][k].shape[0]
            to = fulls[s][k].at[pl.ds(pl.multiple_of(me * depth, 16), depth)]
            here.append(pltpu.make_async_copy(owns[s][k], to, local.at[n]))
            n += 1
    for copy in here:
        copy.start()
    for copy in here:
        copy.wait()
    wait_tr(0, from_tok, tokr)
    ax[...] = nn(px[...], flat(tokr[...]).astype(BF16)).astype(BF16)

    weights_relay(0)
    weights_begin(1)
    wait_tr(1, from_cot, cotr)
    cot_lines = nn(px[...], flat(cotr[...]).astype(BF16))
    cots[...] = cot_lines.reshape(cots.shape).astype(BF16)
    cotz[mine] = cots[mine]
    for d in gz_order:
        gz_copy(1, cots, cotz, d).start()
    weights_end(0)

    rstd_x = project(ax[...].astype(F32), gain_x[...][None], fwx, qkvx)
    weights_relay(1, (0, 1))
    attend_forward(qkvx, probs, mixed, block_x, line_x)
    weights_relay(1, (2, 3))
    mid = ax[...].astype(F32) + nn(mixed[...], fox[...])
    mids[...] = mid.reshape(mids.shape).astype(BF16)
    for d in gz_order:
        gz_copy(0, mids, midr, d).start()
    midr[mine] = mids[mine]
    weights_end(1)

    wait_gz(1, cots, cotz)
    cz = nn(pz[...], flat(cotz[...]).astype(BF16))
    dmix[...] = nt(cz.astype(BF16), foz[...]).astype(BF16)
    wait_gz(0, mids, midr)
    az[...] = nn(pz[...], flat(midr[...]).astype(BF16)).astype(BF16)
    rstd_z = project(az[...].astype(F32), gain_z[...][None], fwz, qkvz)
    attend_backward(qkvz, probs, dmix, joined, block_z, line_z, False)
    cz = nn(pz[...], flat(cotz[...]).astype(BF16))
    back = norm_backward(az[...].astype(F32), cz, rstd_z, gain_z[...][None], joined, fwz, dn)
    grads[...] = tn(pz[...], back).reshape(grads.shape).astype(BF16)
    for d in gz_order:
        gz_copy(2, grads, gradr, d).start()
    gradr[mine] = grads[mine]
    wait_gz(2, grads, gradr)

    dmix[...] = nt(flat(gradr[...]).astype(BF16), fox[...]).astype(BF16)
    attend_backward(qkvx, probs, dmix, joined, block_x, line_x, True)
    back = norm_backward(
        ax[...].astype(F32), flat(gradr[...]), rstd_x, gain_x[...][None], joined, fwx, dn
    )
    outs[...] = tn(px[...], back).reshape(outs.shape).astype(BF16)
    for d in far_first:
        tr_copy(2, from_out, outr, d).start()
    outr[me] = outs[me]
    wait_tr(2, from_out, outr)
    for t in range(nt_):
        out[:, t] = outr[t]


def one_hot(order):
    return jnp.asarray(np.eye(len(order), dtype=np.float32)[order], BF16)


def fits_kernel(trs, gzs, slab, y, x_own, width):
    rows_own = y // trs
    return trs == 4 and rows_own == gzs and (slab * trs * x_own) % 8 == 0 and (rows_own * x_own) % 16 == 0


def fused(trs, gzs, tokens, cotangent, gain_x, wqkv_x, wo_x, gain_z, wqkv_z, wo_z):
    slab, y, x_own, width = tokens.shape
    y_own, x = y // trs, x_own * trs
    rows, z = slab * y * x_own, slab * gzs
    share = rows // gzs
    index = np.arange(rows).reshape(trs, slab, y_own, x_own)
    px = one_hot(index.transpose(2, 1, 0, 3).reshape(-1))
    pz = one_hot(np.arange(rows).reshape(z, x).T.reshape(-1))
    split = (slab, trs, y_own * x_own, width)
    block_x, block_z = 80 if 80 % x == 0 else x, 80 if 80 % z == 0 else z
    tr_slots, gz_slots = (trs, slab, y_own * x_own, width), (gzs, share, width)
    vm = pl.BlockSpec(memory_space=pltpu.VMEM)
    hbm = pl.BlockSpec(memory_space=pl.ANY)
    wide = wqkv_x.shape[1]
    result = pl.pallas_call(
        functools.partial(kernel, trs, gzs, block_x, x, block_z, z),
        out_shape=jax.ShapeDtypeStruct(split, BF16),
        in_specs=[hbm, hbm, vm, hbm, hbm, vm, hbm, hbm, vm, vm],
        out_specs=vm,
        scratch_shapes=[pltpu.VMEM(tr_slots, BF16)] * 4
        + [pltpu.VMEM(gz_slots, BF16)] * 6
        + [pltpu.VMEM((width, wide), BF16), pltpu.VMEM((width, width), BF16)] * 2
        + [pltpu.VMEM((rows, wide), BF16)] * 2
        + [pltpu.VMEM((rows // block_x * H, block_x, block_x), F32)]
        + [pltpu.VMEM((rows, width), BF16)] * 2
        + [pltpu.VMEM((rows, wide), BF16), pltpu.VMEM((rows, width), F32)]
        + [pltpu.VMEM((rows, width), BF16)] * 2
        + [
            pltpu.SemaphoreType.DMA((3, trs)),
            pltpu.SemaphoreType.DMA((3, trs)),
            pltpu.SemaphoreType.DMA((3, gzs)),
            pltpu.SemaphoreType.DMA((3, gzs)),
            pltpu.SemaphoreType.DMA((2, 4, 6)),
            pltpu.SemaphoreType.DMA((2, 4, trs, 2)),
            pltpu.SemaphoreType.DMA((6,)),
        ],
        compiler_params=pltpu.CompilerParams(
            collective_id=0, has_side_effects=True, vmem_limit_bytes=56 * 1024 * 1024
        ),
    )(
        tokens.reshape(split), cotangent.reshape(split),
        gain_x, wqkv_x, wo_x, gain_z, wqkv_z, wo_z, px, pz,
    )
    return result.reshape(tokens.shape)


def solution(mesh):
    trs, gzs = mesh.shape["tr"], mesh.shape["gz"]

    def body(tokens, *rest):
        if fits_kernel(trs, gzs, *tokens.shape):
            return fused(trs, gzs, tokens, *rest)
        return per_device(tokens, *rest)

    return jax.shard_map(
        body,
        mesh=mesh,
        in_specs=(
            P("gz", None, "tr", None),
            P("gz", None, "tr", None),
            P(),
            P("tr", None),
            P("tr", None),
            P(),
            P("tr", None),
            P("tr", None),
        ),
        out_specs=P("gz", None, "tr", None),
        check_vma=False,
    )
```

```python
import functools
import math

import jax
import jax.numpy as jnp
import numpy as np
from jax import lax
from jax.experimental import pallas as pl
from jax.experimental.pallas import tpu as pltpu
from jax.sharding import PartitionSpec as P

H = 6


def head_split(packed, index, model_width):
    piece = packed[..., index * model_width : (index + 1) * model_width]
    return piece.reshape(piece.shape[:-1] + (H, model_width // H))


def merge_heads(value):
    return value.reshape(value.shape[:-2] + (value.shape[-2] * value.shape[-1],))


def recompute(tokens_in, gain_vec, w_in, layout):
    model_width = w_in.shape[0]
    factor = 1.0 / math.sqrt(model_width // H)
    widened = tokens_in.astype(jnp.float32)
    inv_rms = lax.rsqrt(jnp.mean(widened * widened, axis=-1, keepdims=True) + 1e-06)
    normed = (widened * inv_rms * gain_vec).astype(jnp.bfloat16)
    packed = jnp.dot(normed, w_in, preferred_element_type=jnp.float32).astype(jnp.bfloat16)
    queries = head_split(packed, 0, model_width)
    key_part = head_split(packed, 1, model_width)
    values = head_split(packed, 2, model_width)
    key_form = layout.replace("l", "m")
    scores = (
        jnp.einsum(
            layout + "," + key_form + "->bhlm",
            queries,
            key_part,
            preferred_element_type=jnp.float32,
        )
        * factor
    )
    highest = jnp.max(scores, axis=-1, keepdims=True)
    expanded = jnp.exp(scores - highest)
    probs = expanded / jnp.sum(expanded, axis=-1, keepdims=True)
    return (widened, inv_rms, queries, key_part, values, probs, probs.astype(jnp.bfloat16), factor)


def forward_out(tokens_in, gain_vec, w_in, w_out, layout):
    widened, inv_rms, queries, key_part, values, probs, probs_b, factor = recompute(
        tokens_in, gain_vec, w_in, layout
    )
    key_form = layout.replace("l", "m")
    mixed = jnp.einsum(
        "bhlm," + key_form + "->" + layout, probs_b, values, preferred_element_type=jnp.float32
    )
    mixed = merge_heads(mixed.astype(jnp.bfloat16))
    return (widened + jnp.dot(mixed, w_out, preferred_element_type=jnp.float32)).astype(
        jnp.bfloat16
    )


def backward(tokens_in, upstream, gain_vec, w_in, w_out, layout):
    widened, inv_rms, queries, key_part, values, probs, probs_b, factor = recompute(
        tokens_in, gain_vec, w_in, layout
    )
    key_form = layout.replace("l", "m")
    d_mixed = jnp.dot(upstream, w_out.T, preferred_element_type=jnp.float32).astype(jnp.bfloat16)
    d_mixed = d_mixed.reshape(d_mixed.shape[:-1] + (H, d_mixed.shape[-1] // H))
    d_probs = jnp.einsum(
        layout + "," + key_form + "->bhlm", d_mixed, values, preferred_element_type=jnp.float32
    )
    d_values = jnp.einsum(
        "bhlm," + layout + "->" + key_form, probs_b, d_mixed, preferred_element_type=jnp.float32
    ).astype(jnp.bfloat16)
    centre = jnp.sum(probs * d_probs, axis=-1, keepdims=True)
    d_scores = (probs * (d_probs - centre) * factor).astype(jnp.bfloat16)
    d_queries = jnp.einsum(
        "bhlm," + key_form + "->" + layout, d_scores, key_part, preferred_element_type=jnp.float32
    ).astype(jnp.bfloat16)
    d_keys = jnp.einsum(
        "bhlm," + layout + "->" + key_form, d_scores, queries, preferred_element_type=jnp.float32
    ).astype(jnp.bfloat16)
    joined = jnp.concatenate(
        [merge_heads(d_queries), merge_heads(d_keys), merge_heads(d_values)], axis=-1
    )
    d_normed = jnp.dot(joined, w_in.T, preferred_element_type=jnp.float32)
    scaled = d_normed * gain_vec
    d_tokens = inv_rms * (
        scaled - widened * inv_rms * inv_rms * jnp.mean(scaled * widened, axis=-1, keepdims=True)
    )
    return (upstream.astype(jnp.float32) + d_tokens).astype(jnp.bfloat16)


def line_forward(lines, gain_vec, w_in, w_out):
    feature_count = lines.shape[3]
    flat = lines.reshape(-1, lines.shape[2], feature_count)
    return forward_out(flat, gain_vec, w_in, w_out, "blhe").reshape(lines.shape)


def line_backward(lines, upstream, gain_vec, w_in, w_out):
    feature_count = lines.shape[3]
    flat = lines.reshape(-1, lines.shape[2], feature_count)
    flat_up = upstream.reshape(flat.shape)
    return backward(flat, flat_up, gain_vec, w_in, w_out, "blhe").reshape(lines.shape)


def per_device(tokens, cotangent, gain_x, wqkv_x, wo_x, gain_z, wqkv_z, wo_z):
    full_in_x, full_out_x = (
        lax.all_gather(wqkv_x, "tr", axis=0, tiled=True),
        lax.all_gather(wo_x, "tr", axis=0, tiled=True),
    )
    full_in_z, full_out_z = (
        lax.all_gather(wqkv_z, "tr", axis=0, tiled=True),
        lax.all_gather(wo_z, "tr", axis=0, tiled=True),
    )
    width = tokens.shape[-1]
    lines = lax.all_to_all(tokens, "tr", split_axis=1, concat_axis=2, tiled=True)
    cot_lines = lax.all_to_all(cotangent, "tr", split_axis=1, concat_axis=2, tiled=True)
    cells = lines.shape[1] * lines.shape[2]
    flat = (lines.shape[0], cells, width)
    cot_columns = lax.all_to_all(
        cot_lines.reshape(flat), "gz", split_axis=1, concat_axis=0, tiled=True
    )
    mid_lines = line_forward(lines, gain_x, full_in_x, full_out_x)
    mid_columns = lax.all_to_all(
        mid_lines.reshape(flat), "gz", split_axis=1, concat_axis=0, tiled=True
    )
    grad_columns = backward(
        mid_columns, cot_columns, gain_z, full_in_z, full_out_z, "lbhe"
    )
    grad_lines = lax.all_to_all(grad_columns, "gz", split_axis=0, concat_axis=1, tiled=True)
    result_lines = line_backward(lines, grad_lines.reshape(lines.shape), gain_x, full_in_x, full_out_x)
    return lax.all_to_all(result_lines, "tr", split_axis=2, concat_axis=1, tiled=True)


F32, BF16 = jnp.float32, jnp.bfloat16


def nt(a, b):
    return lax.dot_general(a, b, (((1,), (1,)), ((), ())), preferred_element_type=F32)


def tn(a, b):
    return lax.dot_general(a, b, (((0,), (0,)), ((), ())), preferred_element_type=F32)


def nn(a, b):
    return jnp.dot(a, b, preferred_element_type=F32)


def flat(value):
    width = value.shape[-1]
    return value.astype(F32).reshape(-1, width)


def project(a, gain, w, qkv):
    rows, width = a.shape
    rstd = lax.rsqrt(jnp.mean(a * a, axis=-1, keepdims=True) + 1e-06)
    normed = (a * rstd * gain).astype(BF16)

    def part(j, _):
        cols = pl.ds(pl.multiple_of(j * width, width), width)
        qkv[:, cols] = nn(normed, w[:, cols]).astype(BF16)
        return 0

    lax.fori_loop(0, 3, part, 0)
    return rstd


def line_mask(block, line):
    key = lax.broadcasted_iota(jnp.int32, (block, block), 0) // line
    query = lax.broadcasted_iota(jnp.int32, (block, block), 1) // line
    return key == query


def attend_forward(qkv, probs, mixed, block, line):
    rows, width = mixed.shape
    size = width // H
    mask = line_mask(block, line)
    factor = 1.0 / math.sqrt(size)

    def body(b, _):
        at = pl.ds(pl.multiple_of(b * block, block), block)
        for first in range(0, H, 6):
            heads = range(first, first + 6)
            spans = [[pl.ds(n * width + h * size, size) for n in range(3)] for h in heads]
            qk = [nt(qkv[at, sp[1]], qkv[at, sp[0]]) for sp in spans]
            scores = [jnp.where(mask, x * factor, -1e30) for x in qk]
            tops = [jnp.max(x, axis=0, keepdims=True) for x in scores]
            grown = [jnp.exp(x - t) for x, t in zip(scores, tops)]
            sums = [1.0 / jnp.sum(x, axis=0, keepdims=True) for x in grown]
            ps = [x * t for x, t in zip(grown, sums)]
            for h, p in zip(heads, ps):
                probs[b * H + h] = p
            outs = [tn(p.astype(BF16), qkv[at, sp[2]]) for p, sp in zip(ps, spans)]
            for sp, o in zip(spans, outs):
                mixed[at, sp[0]] = o.astype(BF16)
        return 0

    lax.fori_loop(0, rows // block, body, 0, unroll=True)


def attend_backward(qkv, probs, d_mixed, joined, block, line, keep):
    rows, width = d_mixed.shape
    size = width // H
    mask = line_mask(block, line)
    factor = 1.0 / math.sqrt(size)

    def body(b, _):
        at = pl.ds(pl.multiple_of(b * block, block), block)
        for first in range(0, H, 6):
            heads = range(first, first + 6)
            spans = [[pl.ds(n * width + h * size, size) for n in range(3)] for h in heads]
            dps = [nt(qkv[at, sp[2]], d_mixed[at, sp[0]]) for sp in spans]
            if keep:
                ps = [probs[b * H + h] for h in heads]
            else:
                qk = [nt(qkv[at, sp[1]], qkv[at, sp[0]]) for sp in spans]
                scores = [jnp.where(mask, x * factor, -1e30) for x in qk]
                tops = [jnp.max(x, axis=0, keepdims=True) for x in scores]
                grown = [jnp.exp(x - t) for x, t in zip(scores, tops)]
                sums = [1.0 / jnp.sum(x, axis=0, keepdims=True) for x in grown]
                ps = [x * t for x, t in zip(grown, sums)]
            dvs = [nn(p.astype(BF16), d_mixed[at, sp[0]]) for p, sp in zip(ps, spans)]
            centres = [jnp.sum(p * dp, axis=0, keepdims=True) for p, dp in zip(ps, dps)]
            dss = [
                (p * (dp - c) * factor).astype(BF16) for p, dp, c in zip(ps, dps, centres)
            ]
            dks = [nn(ds, qkv[at, sp[0]]) for ds, sp in zip(dss, spans)]
            dqs = [tn(ds, qkv[at, sp[1]]) for ds, sp in zip(dss, spans)]
            for sp, dq, dk, dv in zip(spans, dqs, dks, dvs):
                joined[at, sp[0]] = dq.astype(BF16)
                joined[at, sp[1]] = dk.astype(BF16)
                joined[at, sp[2]] = dv.astype(BF16)
        return 0

    lax.fori_loop(0, rows // block, body, 0, unroll=True)


def norm_backward(a, c, rstd, gain, joined, w, dn):
    width = a.shape[-1]
    for j in range(3):
        part = width // 3
        dn[:, j * part : (j + 1) * part] = nt(joined[...], w[j * part : (j + 1) * part, :])
    scaled = dn[...] * gain
    mean = jnp.mean(scaled * a, axis=-1, keepdims=True)
    return (c + rstd * (scaled - a * (rstd * rstd) * mean)).astype(BF16)


def kernel(
    nt_, ng, block_x, line_x, block_z, line_z,
    tok, cot, gain_x, wx, ox, gain_z, wz, oz, px, pz, out,
    tokr, cotr, outs, outr, mids, midr, cots, cotz, grads, gradr,
    fwx, fox, fwz, foz, qkvx, qkvz, probs, mixed, dmix, joined, dn, ax, az,
    tr_send, tr_recv, gz_send, gz_recv, w_send, w_recv, local,
):
    me, mine = lax.axis_index("tr"), lax.axis_index("gz")
    sib, across = me + 1 - 2 * (me % 2), (me + 2) % nt_
    half = mine % 2
    partner = mine + 1 - 2 * half
    rows, width = ax.shape

    barrier = pltpu.get_barrier_semaphore()
    for d in range(1, nt_):
        pl.semaphore_signal(barrier, inc=1, device_id=((me + d) % nt_, mine), device_id_type=pl.DeviceIdType.MESH)
    for d in range(1, ng):
        pl.semaphore_signal(barrier, inc=1, device_id=(me, (mine + d) % ng), device_id_type=pl.DeviceIdType.MESH)
    pl.semaphore_wait(barrier, nt_ + ng - 2)

    def remote(src, dst, send, recv, t, g):
        return pltpu.make_async_remote_copy(
            src_ref=src, dst_ref=dst, send_sem=send, recv_sem=recv,
            device_id=(t, g), device_id_type=pl.DeviceIdType.MESH,
        )

    def tr_copy(n, source, slots, d):
        t = (me + d) % nt_
        return remote(source(t), slots.at[me], tr_send.at[n, d], tr_recv.at[n, d], t, mine)

    def gz_copy(n, source, slots, d):
        g = (mine + d) % ng
        return remote(source.at[g], slots.at[mine], gz_send.at[n, d], gz_recv.at[n, d], me, g)

    far_first = [2, 3, 1] if nt_ == 4 else list(range(1, nt_))
    gz_order = sorted(range(1, ng), key=lambda d: -min(d, ng - d))

    owns = ((wx, wx, wx, ox), (wz, wz, wz, oz))
    fulls = ((fwx, fwx, fwx, fox), (fwz, fwz, fwz, foz))

    def piece(ref, k, t, h, mine_only):
        depth = ref.shape[0] if mine_only else ref.shape[0] // nt_
        cols = width // 2
        first = h * 3 + k if k < 3 else h
        col = pl.ds(pl.multiple_of(first * cols, 128), cols)
        row = pl.ds(0, depth) if mine_only else pl.ds(pl.multiple_of(t * depth, 16), depth)
        return ref.at[row, col]

    def own_copy(s, k, n, h, t):
        return remote(
            piece(owns[s][k], k, me, h, True), piece(fulls[s][k], k, me, h, False),
            w_send.at[s, k, n], w_recv.at[s, k, me, h], t, mine,
        )

    def relay(s, k, n, h, t, g):
        spot = piece(fulls[s][k], k, across, h, False)
        return remote(spot, spot, w_send.at[s, k, n], w_recv.at[s, k, across, h], t, g)

    def arrive(s, k, src, h):
        spot = piece(fulls[s][k], k, src, h, False)
        remote(spot, spot, w_send.at[s, k, 0], w_recv.at[s, k, src, h], sib, mine).wait_recv()

    def weights_begin(s):
        for k in range(4):
            own_copy(s, k, 2, half, across).start()
        for k in range(4):
            own_copy(s, k, 0, 0, sib).start()
            own_copy(s, k, 1, 1, sib).start()

    def weights_relay(s, pieces=range(4)):
        for k in pieces:
            arrive(s, k, across, half)
            relay(s, k, 3, half, me, partner).start()
            relay(s, k, 4, half, sib, mine).start()

    def weights_end(s):
        far = (sib + 2) % nt_
        for k in range(4):
            arrive(s, k, across, 1 - half)
            relay(s, k, 5, 1 - half, sib, mine).start()
        for k in range(4):
            for h in range(2):
                arrive(s, k, sib, h)
                arrive(s, k, far, h)
            own_copy(s, k, 0, 0, sib).wait_send()
            own_copy(s, k, 1, 1, sib).wait_send()
            own_copy(s, k, 2, half, across).wait_send()
            relay(s, k, 3, half, me, partner).wait_send()
            relay(s, k, 4, half, sib, mine).wait_send()
            relay(s, k, 5, 1 - half, sib, mine).wait_send()

    def wait_tr(n, source, slots):
        for d in range(1, nt_):
            tr_copy(n, source, slots, d).wait_send()
            src = (me + nt_ - d) % nt_
            remote(source(src), slots.at[src], tr_send.at[n, d], tr_recv.at[n, d], src, mine).wait_recv()

    def wait_gz(n, source, slots):
        for d in range(1, ng):
            gz_copy(n, source, slots, d).wait_send()
            src = (mine + ng - d) % ng
            remote(source.at[src], slots.at[src], gz_send.at[n, d], gz_recv.at[n, d], me, src).wait_recv()

    def from_tok(t):
        return tok.at[:, t]

    def from_cot(t):
        return cot.at[:, t]

    def from_out(t):
        return outs.at[t]

    for d in far_first:
        tr_copy(0, from_tok, tokr, d).start()
    weights_begin(0)
    for d in far_first:
        tr_copy(1, from_cot, cotr, d).start()
    here = [pltpu.make_async_copy(tok.at[:, me], tokr.at[me], local.at[0]),
            pltpu.make_async_copy(cot.at[:, me], cotr.at[me], local.at[1])]
    n = 2
    for s in range(2):
        for k in (0, 3):
            depth = owns[s][k].shape[0]
            to = fulls[s][k].at[pl.ds(pl.multiple_of(me * depth, 16), depth)]
            here.append(pltpu.make_async_copy(owns[s][k], to, local.at[n]))
            n += 1
    for copy in here:
        copy.start()
    for copy in here:
        copy.wait()
    wait_tr(0, from_tok, tokr)
    ax[...] = nn(px[...], flat(tokr[...]).astype(BF16)).astype(BF16)

    weights_relay(0)
    weights_begin(1)
    wait_tr(1, from_cot, cotr)
    cot_lines = nn(px[...], flat(cotr[...]).astype(BF16))
    cots[...] = cot_lines.reshape(cots.shape).astype(BF16)
    cotz[mine] = cots[mine]
    for d in gz_order:
        gz_copy(1, cots, cotz, d).start()
    weights_end(0)

    rstd_x = project(ax[...].astype(F32), gain_x[...][None], fwx, qkvx)
    weights_relay(1, (0, 1))
    attend_forward(qkvx, probs, mixed, block_x, line_x)
    weights_relay(1, (2, 3))
    mid = ax[...].astype(F32) + nn(mixed[...], fox[...])
    mids[...] = mid.reshape(mids.shape).astype(BF16)
    for d in gz_order:
        gz_copy(0, mids, midr, d).start()
    midr[mine] = mids[mine]
    weights_end(1)

    wait_gz(1, cots, cotz)
    cz = nn(pz[...], flat(cotz[...]).astype(BF16))
    dmix[...] = nt(cz.astype(BF16), foz[...]).astype(BF16)
    wait_gz(0, mids, midr)
    az[...] = nn(pz[...], flat(midr[...]).astype(BF16)).astype(BF16)
    rstd_z = project(az[...].astype(F32), gain_z[...][None], fwz, qkvz)
    attend_backward(qkvz, probs, dmix, joined, block_z, line_z, False)
    cz = nn(pz[...], flat(cotz[...]).astype(BF16))
    back = norm_backward(az[...].astype(F32), cz, rstd_z, gain_z[...][None], joined, fwz, dn)
    grads[...] = tn(pz[...], back).reshape(grads.shape).astype(BF16)
    for d in gz_order:
        gz_copy(2, grads, gradr, d).start()
    gradr[mine] = grads[mine]
    wait_gz(2, grads, gradr)

    dmix[...] = nt(flat(gradr[...]).astype(BF16), fox[...]).astype(BF16)
    attend_backward(qkvx, probs, dmix, joined, block_x, line_x, True)
    back = norm_backward(
        ax[...].astype(F32), flat(gradr[...]), rstd_x, gain_x[...][None], joined, fwx, dn
    )
    outs[...] = tn(px[...], back).reshape(outs.shape).astype(BF16)
    for d in far_first:
        tr_copy(2, from_out, outr, d).start()
    outr[me] = outs[me]
    wait_tr(2, from_out, outr)
    for t in range(nt_):
        out[:, t] = outr[t]


def one_hot(order):
    return jnp.asarray(np.eye(len(order), dtype=np.float32)[order], BF16)


def fits_kernel(trs, gzs, slab, y, x_own, width):
    rows_own = y // trs
    return trs == 4 and rows_own == gzs and (slab * trs * x_own) % 8 == 0 and (rows_own * x_own) % 16 == 0


def fused(trs, gzs, tokens, cotangent, gain_x, wqkv_x, wo_x, gain_z, wqkv_z, wo_z):
    slab, y, x_own, width = tokens.shape
    y_own, x = y // trs, x_own * trs
    rows, z = slab * y * x_own, slab * gzs
    share = rows // gzs
    index = np.arange(rows).reshape(trs, slab, y_own, x_own)
    px = one_hot(index.transpose(2, 1, 0, 3).reshape(-1))
    pz = one_hot(np.arange(rows).reshape(z, x).T.reshape(-1))
    split = (slab, trs, y_own * x_own, width)
    block_x, block_z = 80 if 80 % x == 0 else x, 80 if 80 % z == 0 else z
    tr_slots, gz_slots = (trs, slab, y_own * x_own, width), (gzs, share, width)
    vm = pl.BlockSpec(memory_space=pltpu.VMEM)
    hbm = pl.BlockSpec(memory_space=pl.ANY)
    wide = wqkv_x.shape[1]
    result = pl.pallas_call(
        functools.partial(kernel, trs, gzs, block_x, x, block_z, z),
        out_shape=jax.ShapeDtypeStruct(split, BF16),
        in_specs=[hbm, hbm, vm, hbm, hbm, vm, hbm, hbm, vm, vm],
        out_specs=vm,
        scratch_shapes=[pltpu.VMEM(tr_slots, BF16)] * 4
        + [pltpu.VMEM(gz_slots, BF16)] * 6
        + [pltpu.VMEM((width, wide), BF16), pltpu.VMEM((width, width), BF16)] * 2
        + [pltpu.VMEM((rows, wide), BF16)] * 2
        + [pltpu.VMEM((rows // block_x * H, block_x, block_x), F32)]
        + [pltpu.VMEM((rows, width), BF16)] * 2
        + [pltpu.VMEM((rows, wide), BF16), pltpu.VMEM((rows, width), F32)]
        + [pltpu.VMEM((rows, width), BF16)] * 2
        + [
            pltpu.SemaphoreType.DMA((3, trs)),
            pltpu.SemaphoreType.DMA((3, trs)),
            pltpu.SemaphoreType.DMA((3, gzs)),
            pltpu.SemaphoreType.DMA((3, gzs)),
            pltpu.SemaphoreType.DMA((2, 4, 6)),
            pltpu.SemaphoreType.DMA((2, 4, trs, 2)),
            pltpu.SemaphoreType.DMA((6,)),
        ],
        compiler_params=pltpu.CompilerParams(
            collective_id=0, has_side_effects=True, vmem_limit_bytes=56 * 1024 * 1024
        ),
    )(
        tokens.reshape(split), cotangent.reshape(split),
        gain_x, wqkv_x, wo_x, gain_z, wqkv_z, wo_z, px, pz,
    )
    return result.reshape(tokens.shape)


def solution(mesh):
    trs, gzs = mesh.shape["tr"], mesh.shape["gz"]

    def body(tokens, *rest):
        if fits_kernel(trs, gzs, *tokens.shape):
            return fused(trs, gzs, tokens, *rest)
        return per_device(tokens, *rest)

    return jax.shard_map(
        body,
        mesh=mesh,
        in_specs=(
            P("gz", None, "tr", None),
            P("gz", None, "tr", None),
            P(),
            P("tr", None),
            P("tr", None),
            P(),
            P("tr", None),
            P("tr", None),
        ),
        out_specs=P("gz", None, "tr", None),
        check_vma=False,
    )
```
